32 devices in a mesh: ctx: 8 (over z, x), head: 4 (over y, core).
Axes of the slice: x: 2, y: 2, z: 4, core: 2. Of those that a mesh axis runs over, the one named last changes fastest.
Arguments:
- query: bfloat16 [16384, 4096], P(('ctx', 'head')), may hold values from -6 to 6
- key: bfloat16 [16384, 2048], P(('ctx', 'head')), may hold values from -6 to 6
- value: bfloat16 [16384, 2048], P(('ctx', 'head')), may hold values from -6 to 6
- out_grad: bfloat16 [16384, 4096], P(('ctx', 'head')), may hold values from -6 to 6
- block_mask: int32 [128, 9], replicated, may hold values from 0 to 1, as said below
Outputs:
- query_grad: bfloat16 [16384, 4096], P(('ctx', 'head'))
- key_grad: bfloat16 [16384, 2048], P(('ctx', 'head'))
- value_grad: bfloat16 [16384, 2048], P(('ctx', 'head'))
The draws below stay inside these ranges and needn't reach their ends.
Inputs may be any that keep to these rules, and one draw needn't show every extreme that they name: block_mask[b, 0] is 1 for every block b; block_mask[b, o] = 1 lets query block b attend key block b - o.
All inputs are finite; a program needn't handle non-finite values.
Results may differ from the reference program's by a relative error of at most 0.0095.
Values may be sent and summed in bfloat16 or wider, within the bound.
No kernel may reach another device: no remote copies, remote signals or barrier semaphores. Data moves between devices by JAX's collectives and lax.ppermute only.
A program may use at most 128 MiB of HBM per device.

```python
import jax
import jax.numpy as jnp
from jax import lax

HQ = 32
KEY_VALUE_HEADS = 16
HEAD_WIDTH = 128
WINDOW = 1024
BLOCK = 128
NOFF = 9
SEQUENCE_TOKENS = 16384
NB = 128


def draw_query(key, part):
    final_output = jnp.clip(jax.random.normal(jax.random.fold_in(key, 1), (SEQUENCE_TOKENS, HQ * HEAD_WIDTH), jnp.float32), -6.0, 6.0)
    return final_output.astype(jnp.bfloat16)


def draw_key(key, part):
    final_output = jnp.clip(jax.random.normal(jax.random.fold_in(key, 2), (SEQUENCE_TOKENS, KEY_VALUE_HEADS * HEAD_WIDTH), jnp.float32), -6.0, 6.0)
    return final_output.astype(jnp.bfloat16)


def draw_block_mask(key, part):
    drawn = (jax.random.randint(jax.random.fold_in(key, 4), (NB, NOFF), 0, 4) < 3).astype(jnp.int32)
    column = jax.lax.broadcasted_iota(jnp.int32, (NB, NOFF), 1)
    return jnp.where(column == 0, 1, drawn).astype(jnp.int32)


def block_scale(key, extent, pieces, low, largest):
    def one(dim, blocks):
        steps = jax.random.uniform(jax.random.fold_in(jax.random.fold_in(key, 6), dim), (blocks,), jnp.float32, low / len(pieces), largest / len(pieces))
        return jnp.repeat(jnp.exp(steps), extent[dim] // blocks).reshape((-1,) + (1,) * (len(extent) - dim - 1))

    loudness = one(*pieces[0])
    for cut in pieces[1:]:
        loudness = loudness * one(*cut)
    return loudness


def normal_values(stream_key, shape, deviation, limit, pieces=(), kind=jnp.bfloat16):
    values = deviation * jax.random.normal(stream_key, shape, jnp.float32)
    if pieces:
        values = values * block_scale(stream_key, shape, pieces, -0.22, 0.18)
    return jnp.clip(values, -limit, limit).astype(kind)


def setup_inputs(seed: int = 0) -> dict:
    arg_keys = jax.random.split(jax.random.key(seed), 6)
    return {
        "query": draw_query(jax.random.fold_in(arg_keys[5], 71), 0),
        "key": draw_key(jax.random.fold_in(arg_keys[5], 71), 0),
        "value": normal_values(arg_keys[2], (SEQUENCE_TOKENS, KEY_VALUE_HEADS * HEAD_WIDTH), 1.0, 6.0, ((0, 32),)),
        "out_grad": normal_values(arg_keys[3], (SEQUENCE_TOKENS, HQ * HEAD_WIDTH), 1.0, 6.0, ((0, 32),)),
        "block_mask": draw_block_mask(jax.random.fold_in(arg_keys[5], 71), 0),
    }


PRE_SCALE = 168.0 ** -0.5


def allowed_mask(mask_rows, n_query, n_key, key_lead, key_first):
    q_index = lax.broadcasted_iota(jnp.int32, (n_query, n_key), 0)
    k_index = lax.broadcasted_iota(jnp.int32, (n_query, n_key), 1)
    gap = key_lead + q_index - k_index
    inside = (gap >= 0) & (gap < WINDOW) & (key_first + k_index >= 0)
    q_blocks = n_query // BLOCK
    k_blocks = n_key // BLOCK
    offsets = mask_rows.shape[1]
    a_index = lax.broadcasted_iota(jnp.int32, (q_blocks, k_blocks, offsets), 0)
    b_index = lax.broadcasted_iota(jnp.int32, (q_blocks, k_blocks, offsets), 1)
    o_index = lax.broadcasted_iota(jnp.int32, (q_blocks, k_blocks, offsets), 2)
    picked = jnp.where(o_index == a_index - b_index + key_lead // BLOCK, mask_rows[:, None, :], 0)
    active = jnp.sum(picked, axis=2) > 0
    active = jnp.repeat(jnp.repeat(active, BLOCK, axis=0), BLOCK, axis=1)
    return inside & active


def scores_of(q_part, k_part, allowed):
    n_query = q_part.shape[0]
    n_key = k_part.shape[0]
    kv_groups = k_part.shape[1] // HEAD_WIDTH
    q_heads = q_part.astype(jnp.float32).reshape(n_query, kv_groups, -1, HEAD_WIDTH)
    k_heads = k_part.astype(jnp.float32).reshape(n_key, kv_groups, HEAD_WIDTH)
    raw_scores = jnp.einsum("qgrd,kgd->grqk", q_heads, k_heads) * PRE_SCALE
    return jnp.where(allowed, raw_scores, -jnp.inf)


def tile_pass(q_part, g_part, k_part, v_part, allowed):
    n_query = q_part.shape[0]
    n_key = k_part.shape[0]
    kv_groups = k_part.shape[1] // HEAD_WIDTH
    scores = scores_of(q_part, k_part, allowed)
    row_max = jnp.max(scores, axis=3, keepdims=True)
    row_total = jnp.sum(jnp.exp(scores - row_max), axis=3, keepdims=True)
    log_total = row_max + jnp.log(row_total)
    probs = jnp.exp(scores - log_total)
    probs_low = probs.astype(jnp.bfloat16).astype(jnp.float32)
    q_heads = q_part.astype(jnp.float32).reshape(n_query, kv_groups, -1, HEAD_WIDTH)
    g_heads = g_part.astype(jnp.float32).reshape(n_query, kv_groups, -1, HEAD_WIDTH)
    k_heads = k_part.astype(jnp.float32).reshape(n_key, kv_groups, HEAD_WIDTH)
    v_heads = v_part.astype(jnp.float32).reshape(n_key, kv_groups, HEAD_WIDTH)
    attended = jnp.einsum("grqk,kgd->qgrd", probs_low, v_heads)
    delta = jnp.transpose(jnp.sum(g_heads * attended, axis=3), (1, 2, 0))
    d_value = jnp.einsum("grqk,qgrd->kgd", probs_low, g_heads)
    d_probs = jnp.einsum("qgrd,kgd->grqk", g_heads, v_heads)
    d_scores = (probs * (d_probs - delta[..., None])).astype(jnp.bfloat16).astype(jnp.float32)
    d_query = jnp.einsum("grqk,kgd->qgrd", d_scores, k_heads) * PRE_SCALE
    d_key = jnp.einsum("grqk,qgrd->kgd", d_scores, q_heads) * PRE_SCALE
    return d_query.reshape(n_query, -1), d_key.reshape(n_key, -1), d_value.reshape(n_key, -1)


def reference(query, key, value, out_grad, block_mask):
    seq_len = query.shape[0]
    tile_rows = BLOCK
    n_tiles = seq_len // tile_rows
    zero_rows = jnp.zeros((WINDOW, key.shape[1]), key.dtype)
    k_ext = jnp.concatenate([zero_rows, key], 0)
    v_ext = jnp.concatenate([zero_rows, value], 0)
    span = tile_rows + WINDOW

    def step_fn(state_pair, tile_index):
        d_key_acc, d_value_acc = state_pair
        first_row = (tile_index * tile_rows).astype(jnp.int32)
        q_part = lax.dynamic_slice_in_dim(query, first_row, tile_rows, 0)
        g_part = lax.dynamic_slice_in_dim(out_grad, first_row, tile_rows, 0)
        k_part = lax.dynamic_slice_in_dim(k_ext, first_row, span, 0)
        v_part = lax.dynamic_slice_in_dim(v_ext, first_row, span, 0)
        mask_rows = lax.dynamic_slice_in_dim(block_mask, (first_row // BLOCK).astype(jnp.int32), tile_rows // BLOCK, 0)
        allowed = allowed_mask(mask_rows, tile_rows, span, WINDOW, first_row - WINDOW)
        d_query, d_key, d_value = tile_pass(q_part, g_part, k_part, v_part, allowed)
        d_key_acc = lax.dynamic_update_slice_in_dim(d_key_acc, lax.dynamic_slice_in_dim(d_key_acc, first_row, span, 0) + d_key, first_row, 0)
        d_value_acc = lax.dynamic_update_slice_in_dim(d_value_acc, lax.dynamic_slice_in_dim(d_value_acc, first_row, span, 0) + d_value, first_row, 0)
        return (d_key_acc, d_value_acc), d_query.astype(jnp.bfloat16)

    tile_ids = jnp.arange(n_tiles, dtype=jnp.int32)
    zero_acc = jnp.zeros((seq_len + WINDOW, key.shape[1]), jnp.float32)
    (d_key_ext, d_value_ext), d_query = lax.scan(step_fn, (zero_acc, zero_acc), tile_ids)
    query_grad = d_query.reshape(seq_len, -1)
    key_grad = d_key_ext[WINDOW:].astype(jnp.bfloat16)
    value_grad = d_value_ext[WINDOW:].astype(jnp.bfloat16)
    return (query_grad, key_grad, value_grad)
```

```python
import functools
import math

import jax
import jax.numpy as jnp
from jax import lax
from jax.experimental import pallas as pl
from jax.experimental.pallas import tpu as pltpu
from jax.sharding import PartitionSpec as P

HEAD_WIDTH = 128
WINDOW = 1024
BLOCK = 128
PRE_SCALE = 168.0 ** (-0.5)
LOG2_SCALE = PRE_SCALE * math.log2(math.e)
AXES = ("ctx", "head")
CHUNKS = 4
NT = (((1,), (1,)), ((), ()))
NN = (((1,), (0,)), ((), ()))


def moved(block, distance):
    n = lax.axis_size(AXES[0]) * lax.axis_size(AXES[1])
    route = [(i, i + distance) for i in range(n) if 0 <= i + distance < n]
    return lax.ppermute(block, AXES, route)


def swapped(block):
    n = lax.axis_size(AXES[0]) * lax.axis_size(AXES[1])
    return lax.ppermute(block, AXES, [(i, i ^ 1) for i in range(n)])


def pack_kernel(k_ref, v_ref, out_ref):
    out_ref[:, :HEAD_WIDTH] = k_ref[...]
    out_ref[:, HEAD_WIDTH:] = v_ref[...]


def packed(key, value, first, heads):
    rows = key.shape[0]
    spec = pl.BlockSpec((rows, HEAD_WIDTH), lambda h: (0, first + h))
    return pl.pallas_call(
        pack_kernel,
        out_shape=jax.ShapeDtypeStruct((rows, heads * 2 * HEAD_WIDTH), key.dtype),
        grid=(heads,),
        in_specs=[spec, spec],
        out_specs=pl.BlockSpec((rows, 2 * HEAD_WIDTH), lambda h: (0, h)),
        name="pack_key_value",
    )(key, value)


def dot(a, b, dims):
    return lax.dot_general(a, b, dims, preferred_element_type=jnp.float32)


def attention_kernel(n_pieces, per_group, chained, *refs):
    bias_ref, q_ref, g_ref, k_ref, v_ref = refs[:5]
    piece_refs = refs[5 : 5 + n_pieces]
    rest = refs[5 + n_pieces + (1 if chained else 0) :]
    dq_ref, down_ref = rest[:2]
    dpiece_refs = rest[2 : 2 + n_pieces]
    k_ext, v_ext, k_turned, q_all, g_all, p_all, ds_all = rest[2 + n_pieces :]
    rows = q_ref.shape[0]
    tiles = rows // BLOCK
    lead = n_pieces * rows
    wide = per_group * BLOCK
    span = WINDOW + BLOCK
    n_off = span // BLOCK
    w = HEAD_WIDTH

    for i, piece in enumerate(piece_refs):
        k_ext[i * rows : (i + 1) * rows, :] = piece[:, :w]
        v_ext[i * rows : (i + 1) * rows, :] = piece[:, w:]
    k_ext[lead:, :] = k_ref[...]
    v_ext[lead:, :] = v_ref[...]
    k_turned[...] = k_ext[...].T
    for b in range(tiles):
        for r in range(per_group):
            at = b * wide + r * BLOCK
            q_all[at : at + BLOCK, :] = q_ref[b * BLOCK : (b + 1) * BLOCK, r * w : (r + 1) * w]
            g_all[at : at + BLOCK, :] = g_ref[b * BLOCK : (b + 1) * BLOCK, r * w : (r + 1) * w]

    k_index = lax.broadcasted_iota(jnp.int32, (BLOCK, wide), 0)
    q_index = lax.rem(lax.broadcasted_iota(jnp.int32, (BLOCK, wide), 1), BLOCK)
    lower = k_index <= q_index

    for b in range(tiles):
        top = b * BLOCK
        cols = slice(b * wide, (b + 1) * wide)
        q_two = q_all[cols, :]
        g_two = g_all[cols, :]
        scores = dot(k_ext[top : top + span, :], q_two, NT)
        parts = [scores[i * BLOCK : (i + 1) * BLOCK] for i in range(n_off)]
        bias = [bias_ref[b, n_off - 1 - i] for i in range(n_off)]
        edge = jnp.where(lower, parts[-1], parts[0] + bias[0])
        inner = parts[1:-1]
        top_score = jnp.max(edge, axis=0, keepdims=True)
        for part, shift in zip(inner, bias[1:-1]):
            top_score = jnp.maximum(top_score, jnp.max(part, axis=0, keepdims=True) + shift)
        top_scaled = top_score * LOG2_SCALE
        weights = [jnp.exp2(edge * LOG2_SCALE - top_scaled)]
        for part, shift in zip(inner, bias[1:-1]):
            weights.append(jnp.exp2(part * LOG2_SCALE - (top_scaled - shift)))
        d_probs = dot(v_ext[top : top + span, :], g_two, NT)
        d_parts = [d_probs[i * BLOCK : (i + 1) * BLOCK] for i in range(n_off)]
        d_parts = [jnp.where(lower, d_parts[-1], d_parts[0])] + d_parts[1:-1]
        total = sum(jnp.sum(x, axis=0, keepdims=True) for x in weights)
        moment = sum(jnp.sum(x * y, axis=0, keepdims=True) for x, y in zip(weights, d_parts))
        inverse = 1.0 / total
        delta = moment * inverse
        for i, (x, y) in enumerate(zip(weights, d_parts)):
            prob = x * inverse
            d_score = prob * (y - delta)
            if i == 0:
                last = slice(top + span - BLOCK, top + span)
                first = slice(top, top + BLOCK)
                p_all[first, cols] = jnp.where(lower, 0.0, prob).astype(jnp.bfloat16)
                p_all[last, cols] = jnp.where(lower, prob, 0.0).astype(jnp.bfloat16)
                ds_all[first, cols] = jnp.where(lower, 0.0, d_score).astype(jnp.bfloat16)
                ds_all[last, cols] = jnp.where(lower, d_score, 0.0).astype(jnp.bfloat16)
            else:
                here = slice(top + i * BLOCK, top + (i + 1) * BLOCK)
                p_all[here, cols] = prob.astype(jnp.bfloat16)
                ds_all[here, cols] = d_score.astype(jnp.bfloat16)
        dq_turned = dot(k_turned[:, top : top + span], ds_all[top : top + span, cols], NN)
        dq_two = dq_turned.T * PRE_SCALE
        for r in range(per_group):
            dq_ref[top : top + BLOCK, r * w : (r + 1) * w] = dq_two[
                r * BLOCK : (r + 1) * BLOCK
            ].astype(dq_ref.dtype)

    n_key = (lead + rows) // BLOCK
    j = 0
    while j < n_key:
        low, high = max(0, j - n_off + 1), min(tiles - 1, j)
        end = j + 1
        while (
            end < n_key
            and (max(0, end - n_off + 1), min(tiles - 1, end)) == (low, high)
            and (end * BLOCK) % rows
        ):
            end += 1
        here = slice(j * BLOCK, end * BLOCK)
        cols = slice(low * wide, (high + 1) * wide)
        dv = dot(p_all[here, cols], g_all[cols, :], NN)
        dk = dot(ds_all[here, cols], q_all[cols, :], NN) * PRE_SCALE
        target = down_ref if j * BLOCK >= lead else dpiece_refs[j * BLOCK // rows]
        at = j * BLOCK % rows
        there = slice(at, at + (end - j) * BLOCK)
        target[there, :w] = dk.astype(target.dtype)
        target[there, w:] = dv.astype(target.dtype)
        j = end


def attention(bias, query, out_grad, key, value, pieces, first, heads, dq_before):
    rows = query.shape[0]
    per_group = query.shape[1] // key.shape[1]
    n = len(pieces)
    w = HEAD_WIDTH
    chained = dq_before is not None
    q_spec = pl.BlockSpec((rows, per_group * w), lambda h: (0, first + h))
    k_spec = pl.BlockSpec((rows, w), lambda h: (0, first + h))
    kv_spec = pl.BlockSpec((rows, 2 * w), lambda h: (0, h))
    in_specs = [pl.BlockSpec(memory_space=pltpu.SMEM), q_spec, q_spec, k_spec, k_spec] + [kv_spec] * n
    operands = [bias, query, out_grad, key, value, *pieces]
    aliases = {}
    if chained:
        aliases = {len(operands): 0}
        in_specs.append(pl.BlockSpec(memory_space=pl.ANY))
        operands.append(dq_before)
    kv_shape = (rows, heads * 2 * w)
    length = (n + 1) * rows
    wide = rows * per_group
    work = heads * wide * (WINDOW + BLOCK)
    bf16 = jnp.bfloat16
    return pl.pallas_call(
        functools.partial(attention_kernel, n, per_group, chained),
        out_shape=[
            jax.ShapeDtypeStruct(query.shape, query.dtype),
            jax.ShapeDtypeStruct(kv_shape, jnp.float32),
        ]
        + [jax.ShapeDtypeStruct(kv_shape, bf16)] * n,
        grid=(heads,),
        in_specs=in_specs,
        out_specs=[q_spec] + [kv_spec] * (n + 1),
        scratch_shapes=[
            pltpu.VMEM((length, w), bf16),
            pltpu.VMEM((length, w), bf16),
            pltpu.VMEM((w, length), bf16),
            pltpu.VMEM((wide, w), bf16),
            pltpu.VMEM((wide, w), bf16),
            pltpu.VMEM((length, wide), bf16),
            pltpu.VMEM((length, wide), bf16),
        ],
        input_output_aliases=aliases,
        compiler_params=pltpu.CompilerParams(vmem_limit_bytes=56 * 1024 * 1024),
        cost_estimate=pl.CostEstimate(
            flops=20 * work * w, bytes_accessed=heads * rows * w * 40, transcendentals=work
        ),
        name="attention_grads",
    )(*operands)


def finish_kernel(n, keep_refs, own_ref, *refs):
    dk_ref, dv_ref = refs[-2:]
    total = own_ref[...]
    for keep, ref in zip(keep_refs, refs[:n]):
        total = total + ref[...].astype(jnp.float32)
    w = HEAD_WIDTH
    dk_ref[...] = total[:, :w].astype(dk_ref.dtype)
    dv_ref[...] = total[:, w:].astype(dv_ref.dtype)


def finished(own, terms, first, heads, shape, before):
    rows = own.shape[0]
    w = HEAD_WIDTH
    kv_spec = pl.BlockSpec((rows, 2 * w), lambda h: (0, h))
    out_spec = pl.BlockSpec((rows, w), lambda h: (0, first + h))
    operands = [own, *terms]
    in_specs = [kv_spec] * len(operands)
    aliases = {}
    if before is not None:
        aliases = {len(operands): 0, len(operands) + 1: 1}
        operands += list(before)
        in_specs += [pl.BlockSpec(memory_space=pl.ANY)] * 2
    return pl.pallas_call(
        functools.partial(finish_kernel, len(terms), [True] * len(terms)),
        out_shape=[jax.ShapeDtypeStruct(shape, jnp.bfloat16)] * 2,
        grid=(heads,),
        in_specs=in_specs,
        out_specs=[out_spec] * 2,
        input_output_aliases=aliases,
        name="sum_key_value_grads",
    )(*operands)


def on_device(query, key, value, out_grad, block_mask):
    rows = query.shape[0]
    kv_heads = key.shape[1] // HEAD_WIDTH
    n_pieces = WINDOW // rows
    n_head = lax.axis_size("head")
    device = lax.axis_index("ctx") * n_head + lax.axis_index("head")
    first_block = device * (rows // BLOCK)
    own_rows = lax.dynamic_slice_in_dim(block_mask, first_block, rows // BLOCK, 0)
    block = first_block + lax.broadcasted_iota(jnp.int32, own_rows.shape, 0)
    offset = lax.broadcasted_iota(jnp.int32, own_rows.shape, 1)
    usable = (own_rows > 0) & (block >= offset)
    bias = jnp.where(usable, 0.0, -jnp.inf).astype(jnp.float32)
    paired = n_pieces == 2 and n_head % 2 == 0
    odd = lax.rem(device, 2) == 1

    n_chunks = CHUNKS if kv_heads % CHUNKS == 0 else 1
    heads = kv_heads // n_chunks
    bf16 = jnp.bfloat16
    f32 = jnp.float32

    packs = [packed(key, value, i * heads, heads) for i in range(n_chunks)]
    if paired:
        far = [moved(x, 2) for x in packs]
        near = [swapped(jnp.where(odd, x, y)) for x, y in zip(far, packs)]
        pieces = [[x, y] for x, y in zip(far, near)]
    else:
        pieces = [[moved(x, j) for j in range(n_pieces, 0, -1)] for x in packs]

    dq = None
    grads = None
    for i in range(n_chunks):
        out = attention(bias, query, out_grad, key, value, pieces[i], i * heads, heads, dq)
        dq, own = out[:2]
        if paired:
            d_far, d_near = out[2:]
            from_pair = swapped(d_near)
            for_far = jnp.where(odd, d_far.astype(f32) + from_pair.astype(f32), d_far.astype(f32))
            back = moved(for_far.astype(bf16), -2)
            pair_term = jnp.where(odd, jnp.zeros_like(from_pair), from_pair)
            terms = [back, pair_term]
        else:
            terms = [moved(x, j - n_pieces) for j, x in enumerate(out[2:])]
        grads = finished(own, terms, i * heads, heads, key.shape, grads)
    return (dq, grads[0], grads[1])


def solution(mesh):
    split = P(("ctx", "head"), None)
    return jax.shard_map(
        on_device,
        mesh=mesh,
        in_specs=(split, split, split, split, P()),
        out_specs=(split, split, split),
        check_vma=False,
    )
```

```python
import functools
import math

import jax
import jax.numpy as jnp
from jax import lax
from jax.experimental import pallas as pl
from jax.experimental.pallas import tpu as pltpu
from jax.sharding import PartitionSpec as P

HEAD_WIDTH = 128
WINDOW = 1024
BLOCK = 128
PRE_SCALE = 168.0 ** (-0.5)
LOG2_SCALE = PRE_SCALE * math.log2(math.e)
AXES = ("ctx", "head")
CHUNK_SHARES = (3, 3, 3, 2, 2, 2, 1)
NT = (((1,), (1,)), ((), ()))
NN = (((1,), (0,)), ((), ()))


def moved(block, distance):
    n = lax.axis_size(AXES[0]) * lax.axis_size(AXES[1])
    route = [(i, i + distance) for i in range(n) if 0 <= i + distance < n]
    return lax.ppermute(block, AXES, route)


def swapped(block):
    n = lax.axis_size(AXES[0]) * lax.axis_size(AXES[1])
    return lax.ppermute(block, AXES, [(i, i ^ 1) for i in range(n)])


def pack_kernel(k_ref, v_ref, *refs):
    out_ref = refs[-1]
    out_ref[:, :HEAD_WIDTH] = k_ref[...]
    out_ref[:, HEAD_WIDTH:] = v_ref[...]


def packed(key, value, first, heads, after):
    rows = key.shape[0]
    spec = pl.BlockSpec((rows, HEAD_WIDTH), lambda h: (0, first + h))
    return pl.pallas_call(
        pack_kernel,
        out_shape=jax.ShapeDtypeStruct((rows, heads * 2 * HEAD_WIDTH), key.dtype),
        grid=(heads,),
        in_specs=[spec, spec] + [pl.BlockSpec(memory_space=pl.ANY)] * len(after),
        out_specs=pl.BlockSpec((rows, 2 * HEAD_WIDTH), lambda h: (0, h)),
        name="pack_key_value",
    )(key, value, *after)


def dot(a, b, dims):
    return lax.dot_general(a, b, dims, preferred_element_type=jnp.float32)


def attention_kernel(n_pieces, per_group, n_extra, *refs):
    flag_ref, bias_ref, q_ref, g_ref, k_ref, v_ref = refs[:6]
    piece_refs = refs[6 : 6 + n_pieces]
    rest = refs[6 + n_pieces + n_extra :]
    dq_ref, flag_out_ref, down_ref = rest[:3]
    dpiece_refs = rest[3 : 3 + n_pieces]
    k_ext, v_ext, k_turned, q_all, g_all, p_all, ds_all = rest[3 + n_pieces :]
    flag_out_ref[0, 0] = flag_ref[0, 0]
    rows = q_ref.shape[0]
    tiles = rows // BLOCK
    lead = n_pieces * rows
    wide = per_group * BLOCK
    span = WINDOW + BLOCK
    n_off = span // BLOCK
    w = HEAD_WIDTH

    for i, piece in enumerate(piece_refs):
        k_ext[i * rows : (i + 1) * rows, :] = piece[:, :w]
        v_ext[i * rows : (i + 1) * rows, :] = piece[:, w:]
    k_ext[lead:, :] = k_ref[...]
    v_ext[lead:, :] = v_ref[...]
    k_turned[...] = k_ext[...].T
    for b in range(tiles):
        for r in range(per_group):
            at = b * wide + r * BLOCK
            q_all[at : at + BLOCK, :] = q_ref[b * BLOCK : (b + 1) * BLOCK, r * w : (r + 1) * w]
            g_all[at : at + BLOCK, :] = g_ref[b * BLOCK : (b + 1) * BLOCK, r * w : (r + 1) * w]

    k_index = lax.broadcasted_iota(jnp.int32, (BLOCK, wide), 0)
    q_index = lax.rem(lax.broadcasted_iota(jnp.int32, (BLOCK, wide), 1), BLOCK)
    lower = k_index <= q_index

    for b in range(tiles):
        top = b * BLOCK
        cols = slice(b * wide, (b + 1) * wide)
        q_two = q_all[cols, :]
        g_two = g_all[cols, :]
        scores = dot(k_ext[top : top + span, :], q_two, NT)
        parts = [scores[i * BLOCK : (i + 1) * BLOCK] for i in range(n_off)]
        bias = [bias_ref[b, n_off - 1 - i] for i in range(n_off)]
        edge = jnp.where(lower, parts[-1], parts[0] + bias[0])
        inner = parts[1:-1]
        top_score = jnp.max(edge, axis=0, keepdims=True)
        for part, shift in zip(inner, bias[1:-1]):
            top_score = jnp.maximum(top_score, jnp.max(part, axis=0, keepdims=True) + shift)
        top_scaled = top_score * LOG2_SCALE
        weights = [jnp.exp2(edge * LOG2_SCALE - top_scaled)]
        for part, shift in zip(inner, bias[1:-1]):
            weights.append(jnp.exp2(part * LOG2_SCALE - (top_scaled - shift)))
        d_probs = dot(v_ext[top : top + span, :], g_two, NT)
        d_parts = [d_probs[i * BLOCK : (i + 1) * BLOCK] for i in range(n_off)]
        d_parts = [jnp.where(lower, d_parts[-1], d_parts[0])] + d_parts[1:-1]
        total = sum(jnp.sum(x, axis=0, keepdims=True) for x in weights)
        moment = sum(jnp.sum(x * y, axis=0, keepdims=True) for x, y in zip(weights, d_parts))
        inverse = 1.0 / total
        delta = moment * inverse
        for i, (x, y) in enumerate(zip(weights, d_parts)):
            prob = x * inverse
            d_score = prob * (y - delta)
            if i == 0:
                last = slice(top + span - BLOCK, top + span)
                first = slice(top, top + BLOCK)
                p_all[first, cols] = jnp.where(lower, 0.0, prob).astype(jnp.bfloat16)
                p_all[last, cols] = jnp.where(lower, prob, 0.0).astype(jnp.bfloat16)
                ds_all[first, cols] = jnp.where(lower, 0.0, d_score).astype(jnp.bfloat16)
                ds_all[last, cols] = jnp.where(lower, d_score, 0.0).astype(jnp.bfloat16)
            else:
                here = slice(top + i * BLOCK, top + (i + 1) * BLOCK)
                p_all[here, cols] = prob.astype(jnp.bfloat16)
                ds_all[here, cols] = d_score.astype(jnp.bfloat16)
        dq_turned = dot(k_turned[:, top : top + span], ds_all[top : top + span, cols], NN)
        dq_two = dq_turned.T * PRE_SCALE
        for r in range(per_group):
            dq_ref[top : top + BLOCK, r * w : (r + 1) * w] = dq_two[
                r * BLOCK : (r + 1) * BLOCK
            ].astype(dq_ref.dtype)

    n_key = (lead + rows) // BLOCK
    j = 0
    while j < n_key:
        low, high = max(0, j - n_off + 1), min(tiles - 1, j)
        end = j + 1
        while (
            end < n_key
            and (max(0, end - n_off + 1), min(tiles - 1, end)) == (low, high)
            and (end * BLOCK) % rows
        ):
            end += 1
        here = slice(j * BLOCK, end * BLOCK)
        cols = slice(low * wide, (high + 1) * wide)
        dv = dot(p_all[here, cols], g_all[cols, :], NN)
        dk = dot(ds_all[here, cols], q_all[cols, :], NN) * PRE_SCALE
        target = down_ref if j * BLOCK >= lead else dpiece_refs[j * BLOCK // rows]
        at = j * BLOCK % rows
        there = slice(at, at + (end - j) * BLOCK)
        target[there, :w] = dk.astype(target.dtype)
        target[there, w:] = dv.astype(target.dtype)
        j = end


def attention(flag, bias, query, out_grad, key, value, pieces, first, heads, dq_before, after):
    rows = query.shape[0]
    per_group = query.shape[1] // key.shape[1]
    n = len(pieces)
    w = HEAD_WIDTH
    q_spec = pl.BlockSpec((rows, per_group * w), lambda h: (0, first + h))
    k_spec = pl.BlockSpec((rows, w), lambda h: (0, first + h))
    kv_spec = pl.BlockSpec((rows, 2 * w), lambda h: (0, h))
    scalars = pl.BlockSpec(memory_space=pltpu.SMEM)
    in_specs = [scalars, scalars, q_spec, q_spec, k_spec, k_spec] + [kv_spec] * n
    operands = [flag, bias, query, out_grad, key, value, *pieces]
    aliases = {}
    if dq_before is not None:
        aliases = {len(operands): 0}
        operands.append(dq_before)
    operands += after
    n_extra = len(operands) - len(in_specs)
    in_specs += [pl.BlockSpec(memory_space=pl.ANY)] * n_extra
    kv_shape = (rows, heads * 2 * w)
    length = (n + 1) * rows
    wide = rows * per_group
    bf16 = jnp.bfloat16
    return pl.pallas_call(
        functools.partial(attention_kernel, n, per_group, n_extra),
        out_shape=[
            jax.ShapeDtypeStruct(query.shape, query.dtype),
            jax.ShapeDtypeStruct(flag.shape, flag.dtype),
            jax.ShapeDtypeStruct(kv_shape, jnp.float32),
        ]
        + [jax.ShapeDtypeStruct(kv_shape, bf16)] * n,
        grid=(heads,),
        in_specs=in_specs,
        out_specs=[q_spec, scalars] + [kv_spec] * (n + 1),
        scratch_shapes=[
            pltpu.VMEM((length, w), bf16),
            pltpu.VMEM((length, w), bf16),
            pltpu.VMEM((w, length), bf16),
            pltpu.VMEM((wide, w), bf16),
            pltpu.VMEM((wide, w), bf16),
            pltpu.VMEM((length, wide), bf16),
            pltpu.VMEM((length, wide), bf16),
        ],
        input_output_aliases=aliases,
        compiler_params=pltpu.CompilerParams(vmem_limit_bytes=56 * 1024 * 1024),
        cost_estimate=pl.CostEstimate(flops=heads * 1_000_000, bytes_accessed=1, transcendentals=0),
        name="attention_grads",
    )(*operands)


def finish_kernel(n, own_ref, *refs):
    dk_ref, dv_ref = refs[-2:]
    total = own_ref[...]
    for ref in refs[:n]:
        total = total + ref[...].astype(jnp.float32)
    w = HEAD_WIDTH
    dk_ref[...] = total[:, :w].astype(dk_ref.dtype)
    dv_ref[...] = total[:, w:].astype(dv_ref.dtype)


def finished(own, terms, first, heads, shape, before, after):
    rows = own.shape[0]
    w = HEAD_WIDTH
    kv_spec = pl.BlockSpec((rows, 2 * w), lambda h: (0, h))
    out_spec = pl.BlockSpec((rows, w), lambda h: (0, first + h))
    operands = [own, *terms]
    in_specs = [kv_spec] * len(operands)
    aliases = {}
    if before is not None:
        aliases = {len(operands): 0, len(operands) + 1: 1}
        operands += list(before)
    operands += after
    in_specs += [pl.BlockSpec(memory_space=pl.ANY)] * (len(operands) - len(in_specs))
    return pl.pallas_call(
        functools.partial(finish_kernel, len(terms)),
        out_shape=[jax.ShapeDtypeStruct(shape, jnp.bfloat16)] * 2,
        grid=(heads,),
        in_specs=in_specs,
        out_specs=[out_spec] * 2,
        input_output_aliases=aliases,
        name="sum_key_value_grads",
    )(*operands)


def chunk_heads(kv_heads):
    total = sum(CHUNK_SHARES)
    if kv_heads % total:
        return [kv_heads]
    return [share * kv_heads // total for share in CHUNK_SHARES]


def on_device(query, key, value, out_grad, block_mask):
    rows = query.shape[0]
    kv_heads = key.shape[1] // HEAD_WIDTH
    n_pieces = WINDOW // rows
    n_head = lax.axis_size("head")
    device = lax.axis_index("ctx") * n_head + lax.axis_index("head")
    first_block = device * (rows // BLOCK)
    own_rows = lax.dynamic_slice_in_dim(block_mask, first_block, rows // BLOCK, 0)
    block = first_block + lax.broadcasted_iota(jnp.int32, own_rows.shape, 0)
    offset = lax.broadcasted_iota(jnp.int32, own_rows.shape, 1)
    usable = (own_rows > 0) & (block >= offset)
    bias = jnp.where(usable, 0.0, -jnp.inf).astype(jnp.float32)
    paired = n_pieces == 2 and n_head % 2 == 0
    flag = lax.rem(device, 2).astype(jnp.int32).reshape(1, 1)
    bf16 = jnp.bfloat16
    f32 = jnp.float32

    counts = chunk_heads(kv_heads)
    n_chunks = len(counts)
    firsts = [sum(counts[:i]) for i in range(n_chunks)]
    packs = []
    for first, heads in zip(firsts, counts):
        packs.append(packed(key, value, first, heads, packs[-1:]))
    if paired:
        far = [moved(x, 2) for x in packs]
    else:
        far = [[moved(x, j) for j in range(n_pieces, 0, -1)] for x in packs]

    def offer(i):
        return jnp.where(flag[0, 0] == 1, far[i], packs[i])

    def settle(i):
        odd = flag[0, 0] == 1
        d_far, from_pair = waiting[i]
        for_far = d_far.astype(f32) + jnp.where(odd, from_pair, 0).astype(f32)
        for_far = for_far.astype(bf16)
        for_near = jnp.where(odd, 0, from_pair).astype(bf16)
        terms.append([moved(for_far, -2), for_near])
        return for_far

    dq = None
    owns, terms, waiting, offers, nears = [], [], [], [], []
    for i in range(n_chunks):
        after = []
        if paired:
            for j in range(len(offers), min(i + 2, n_chunks)):
                offers.append(offer(j))
                nears.append(swapped(offers[j]))
                after.append(offers[j])
            if i >= 2:
                after.append(settle(i - 2))
            if i >= 4:
                after.append(terms[i - 4][0])
        pieces = [far[i], nears[i]] if paired else far[i]
        dq, flag, own, *d_pieces = attention(
            flag, bias, query, out_grad, key, value, pieces, firsts[i], counts[i], dq, after
        )
        owns.append(own)
        if paired:
            waiting.append([d_pieces[0], swapped(d_pieces[1])])
        else:
            terms.append([moved(x, j - n_pieces) for j, x in enumerate(d_pieces)])
    last = []
    if paired:
        for i in range(len(terms), n_chunks):
            last = [settle(i)]
    grads = None
    for i in range(n_chunks):
        hold = last if i < n_chunks - 1 else []
        grads = finished(owns[i], terms[i], firsts[i], counts[i], key.shape, grads, hold)
    return (dq, grads[0], grads[1])


def solution(mesh):
    split = P(("ctx", "head"), None)
    return jax.shard_map(
        on_device,
        mesh=mesh,
        in_specs=(split, split, split, split, P()),
        out_specs=(split, split, split),
        check_vma=False,
    )
```

```python
import functools
import math

import jax
import jax.numpy as jnp
from jax import lax
from jax.experimental import pallas as pl
from jax.experimental.pallas import tpu as pltpu
from jax.sharding import PartitionSpec as P

HEAD_WIDTH = 128
WINDOW = 1024
BLOCK = 128
PRE_SCALE = 168.0 ** (-0.5)
LOG2_SCALE = PRE_SCALE * math.log2(math.e)
AXES = ("ctx", "head")
CHUNK_SHARES = (4, 4, 4, 2, 2)
HEADS_PER_STEP = 2
NT = (((1,), (1,)), ((), ()))
NN = (((1,), (0,)), ((), ()))


def moved(block, distance):
    n = lax.axis_size(AXES[0]) * lax.axis_size(AXES[1])
    route = [(i, i + distance) for i in range(n) if 0 <= i + distance < n]
    return lax.ppermute(block, AXES, route)


def swapped(block):
    n = lax.axis_size(AXES[0]) * lax.axis_size(AXES[1])
    return lax.ppermute(block, AXES, [(i, i ^ 1) for i in range(n)])


def pack_kernel(counts, k_ref, v_ref, *out_refs):
    w = HEAD_WIDTH
    at = 0
    for heads, out_ref in zip(counts, out_refs):
        for h in range(heads):
            source = slice((at + h) * w, (at + h + 1) * w)
            out_ref[:, 2 * h * w : (2 * h + 1) * w] = k_ref[:, source]
            out_ref[:, (2 * h + 1) * w : (2 * h + 2) * w] = v_ref[:, source]
        at += heads


def packed(key, value, counts):
    rows, width = key.shape
    step = min(rows, BLOCK)
    spec = pl.BlockSpec((step, width), lambda r: (r, 0))
    widths = [2 * HEAD_WIDTH * heads for heads in counts]
    return pl.pallas_call(
        functools.partial(pack_kernel, counts),
        out_shape=[jax.ShapeDtypeStruct((rows, x), key.dtype) for x in widths],
        grid=(rows // step,),
        in_specs=[spec, spec],
        out_specs=[pl.BlockSpec((step, x), lambda r: (r, 0)) for x in widths],
        name="pack_key_value",
    )(key, value)


def dot(a, b, dims):
    return lax.dot_general(a, b, dims, preferred_element_type=jnp.float32)


def attention_kernel(n_pieces, per_group, per_step, n_extra, *refs):
    flag_ref, bias_ref, q_ref, g_ref, k_ref, v_ref = refs[:6]
    piece_refs = refs[6 : 6 + n_pieces]
    rest = refs[6 + n_pieces + n_extra :]
    dq_ref, flag_out_ref, down_ref = rest[:3]
    dpiece_refs = rest[3 : 3 + n_pieces]
    k_ext, v_ext, k_turned, q_all, g_all, q_low, g_low, p_all, ds_all = rest[3 + n_pieces :]
    flag_out_ref[0, 0] = flag_ref[0, 0]
    rows = q_ref.shape[0]
    tiles = rows // BLOCK
    lead = n_pieces * rows
    wide = per_group * BLOCK
    span = WINDOW + BLOCK
    n_off = span // BLOCK
    w = HEAD_WIDTH
    bf16 = jnp.bfloat16

    for s in range(per_step):
        for i, piece in enumerate(piece_refs):
            k_ext[s, i * rows : (i + 1) * rows, :] = piece[:, 2 * s * w : (2 * s + 1) * w]
            v_ext[s, i * rows : (i + 1) * rows, :] = piece[:, (2 * s + 1) * w : (2 * s + 2) * w]
        k_ext[s, lead:, :] = k_ref[:, s * w : (s + 1) * w]
        v_ext[s, lead:, :] = v_ref[:, s * w : (s + 1) * w]
        k_turned[s] = k_ext[s].T
        for b in range(tiles):
            for r in range(per_group):
                at = b * wide + r * BLOCK
                source = (
                    slice(b * BLOCK, (b + 1) * BLOCK),
                    slice((s * per_group + r) * w, (s * per_group + r + 1) * w),
                )
                q_all[s, at : at + BLOCK, :] = q_ref[source]
                g_all[s, at : at + BLOCK, :] = g_ref[source]

    k_index = lax.broadcasted_iota(jnp.int32, (BLOCK, wide), 0)
    q_index = lax.rem(lax.broadcasted_iota(jnp.int32, (BLOCK, wide), 1), BLOCK)
    lower = k_index <= q_index
    group = 3 * BLOCK if n_off % 3 == 0 else BLOCK
    units = [(s, b) for s in range(per_step) for b in range(tiles)]

    def group_steps(u, key_ref, query_ref, parts):
        s, b = units[u]

        def one(start):
            top = b * BLOCK + start
            out = dot(key_ref[s, top : top + group, :], query_ref[s, b * wide : (b + 1) * wide, :], NT)
            parts.extend(out[i * BLOCK : (i + 1) * BLOCK] for i in range(group // BLOCK))

        return [functools.partial(one, start) for start in range(0, span, group)]

    def folded(x, op):
        return op(x.reshape(BLOCK // 8, 8, wide), axis=0)

    def edge_first(parts, bias0):
        first = parts[0] if bias0 is None else parts[0] + bias0
        return [jnp.where(lower, parts[-1], first)] + parts[1:-1]

    def key_steps(s):
        n_key = (lead + rows) // BLOCK
        steps = []

        def one(j, end, low, high):
            here = slice(j * BLOCK, end * BLOCK)
            cols = slice(low * wide, (high + 1) * wide)
            dv = dot(p_all[s, here, cols], g_low[s, cols, :], NN)
            dk = dot(ds_all[s, here, cols], q_low[s, cols, :], NN) * PRE_SCALE
            for i in range(j, end):
                target = down_ref if i * BLOCK >= lead else dpiece_refs[i * BLOCK // rows]
                there = slice(i * BLOCK % rows, i * BLOCK % rows + BLOCK)
                part = slice((i - j) * BLOCK, (i - j + 1) * BLOCK)
                target[there, 2 * s * w : (2 * s + 1) * w] = dk[part].astype(target.dtype)
                target[there, (2 * s + 1) * w : (2 * s + 2) * w] = dv[part].astype(target.dtype)

        j = 0
        while j < n_key:
            use = max(0, j - n_off + 1), min(tiles - 1, j)
            end = j + 1
            while end < n_key and (max(0, end - n_off + 1), min(tiles - 1, end)) == use:
                end += 1
            steps.append(functools.partial(one, j, end, *use))
            j = end
        return steps

    pending = []
    scores = [[] for _ in units]
    d_probs = [[] for _ in units]
    for step in group_steps(0, k_ext, q_all, scores[0]) + group_steps(0, v_ext, g_all, d_probs[0]):
        step()

    for u, (s, b) in enumerate(units):
        top = b * BLOCK
        cols = slice(b * wide, (b + 1) * wide)
        ahead = group_steps(u + 1, k_ext, q_all, scores[u + 1]) if u + 1 < len(units) else []
        later = group_steps(u + 1, v_ext, g_all, d_probs[u + 1]) if u + 1 < len(units) else []
        bias = [bias_ref[b, n_off - 1 - i] for i in range(n_off - 1)]
        parts = edge_first(scores[u], bias[0])
        shifts = [None] + bias[1:]
        best = folded(parts[0], jnp.max)
        for part, shift in zip(parts[1:], shifts[1:]):
            best = jnp.maximum(best, folded(part, jnp.max) + shift)
        best = jnp.max(best, axis=0, keepdims=True) * LOG2_SCALE
        d_parts = edge_first(d_probs[u], None)
        total = jnp.zeros((8, wide), jnp.float32)
        moment = jnp.zeros((8, wide), jnp.float32)
        weights = []
        for i, (part, d_part, shift) in enumerate(zip(parts, d_parts, shifts)):
            if i % 3 == 0 and ahead:
                ahead.pop(0)()
            if i % 3 == 1 and pending:
                pending.pop(0)()
            x = jnp.exp2(part * LOG2_SCALE - (best if shift is None else best - shift))
            weights.append(x)
            total = total + folded(x, jnp.sum)
            moment = moment + folded(x * d_part, jnp.sum)
            if i == 0:
                p_all[s, top : top + BLOCK, cols] = jnp.where(lower, 0.0, x).astype(bf16)
                p_all[s, top + WINDOW : top + span, cols] = jnp.where(lower, x, 0.0).astype(bf16)
            else:
                p_all[s, top + i * BLOCK : top + (i + 1) * BLOCK, cols] = x.astype(bf16)
        for step in ahead:
            step()
        inverse = 1.0 / jnp.sum(total, axis=0, keepdims=True)
        delta = jnp.sum(moment, axis=0, keepdims=True) * inverse
        column = jnp.broadcast_to(inverse, (8, wide)).T[:, :1]
        q_low[s, cols, :] = (q_all[s, cols, :].astype(jnp.float32) * column).astype(bf16)
        g_low[s, cols, :] = (g_all[s, cols, :].astype(jnp.float32) * column).astype(bf16)
        for i, (x, d_part) in enumerate(zip(weights, d_parts)):
            if i % 3 == 0 and later:
                later.pop(0)()
            if i % 3 == 1 and pending:
                pending.pop(0)()
            d_score = x * (d_part - delta)
            if i == 0:
                ds_all[s, top : top + BLOCK, cols] = jnp.where(lower, 0.0, d_score).astype(bf16)
                ds_all[s, top + WINDOW : top + span, cols] = jnp.where(lower, d_score, 0.0).astype(
                    bf16
                )
            else:
                ds_all[s, top + i * BLOCK : top + (i + 1) * BLOCK, cols] = d_score.astype(bf16)
        for step in later:
            step()
        scores[u] = d_probs[u] = None

        def query_step(s=s, top=top, cols=cols, inverse=inverse):
            turned = dot(k_turned[s, :, top : top + span], ds_all[s, top : top + span, cols], NN)
            dq_two = (turned * (inverse * PRE_SCALE)).T
            for r in range(per_group):
                at = (s * per_group + r) * w
                dq_ref[top : top + BLOCK, at : at + w] = dq_two[
                    r * BLOCK : (r + 1) * BLOCK
                ].astype(dq_ref.dtype)

        pending.append(query_step)
        if b == tiles - 1:
            pending += key_steps(s)
    for step in pending:
        step()


def attention(flag, bias, query, out_grad, key, value, pieces, first, heads, dq_before, after):
    rows = query.shape[0]
    per_group = query.shape[1] // key.shape[1]
    n = len(pieces)
    w = HEAD_WIDTH
    per_step = next(x for x in (HEADS_PER_STEP, 1) if heads % x == 0 and first % x == 0)
    at = first // per_step
    q_spec = pl.BlockSpec((rows, per_step * per_group * w), lambda h: (0, at + h))
    k_spec = pl.BlockSpec((rows, per_step * w), lambda h: (0, at + h))
    kv_spec = pl.BlockSpec((rows, per_step * 2 * w), lambda h: (0, h))
    scalars = pl.BlockSpec(memory_space=pltpu.SMEM)
    in_specs = [scalars, scalars, q_spec, q_spec, k_spec, k_spec] + [kv_spec] * n
    operands = [flag, bias, query, out_grad, key, value, *pieces]
    aliases = {}
    if dq_before is not None:
        aliases = {len(operands): 0}
        operands.append(dq_before)
    operands += after
    n_extra = len(operands) - len(in_specs)
    in_specs += [pl.BlockSpec(memory_space=pl.ANY)] * n_extra
    kv_shape = (rows, heads * 2 * w)
    length = (n + 1) * rows
    wide = rows * per_group
    bf16 = jnp.bfloat16
    return pl.pallas_call(
        functools.partial(attention_kernel, n, per_group, per_step, n_extra),
        out_shape=[
            jax.ShapeDtypeStruct(query.shape, query.dtype),
            jax.ShapeDtypeStruct(flag.shape, flag.dtype),
            jax.ShapeDtypeStruct(kv_shape, jnp.float32),
        ]
        + [jax.ShapeDtypeStruct(kv_shape, bf16)] * n,
        grid=(heads // per_step,),
        in_specs=in_specs,
        out_specs=[q_spec, scalars] + [kv_spec] * (n + 1),
        scratch_shapes=[
            pltpu.VMEM((per_step, length, w), bf16),
            pltpu.VMEM((per_step, length, w), bf16),
            pltpu.VMEM((per_step, w, length), bf16),
            pltpu.VMEM((per_step, wide, w), bf16),
            pltpu.VMEM((per_step, wide, w), bf16),
            pltpu.VMEM((per_step, wide, w), bf16),
            pltpu.VMEM((per_step, wide, w), bf16),
            pltpu.VMEM((per_step, length, wide), bf16),
            pltpu.VMEM((per_step, length, wide), bf16),
        ],
        input_output_aliases=aliases,
        compiler_params=pltpu.CompilerParams(vmem_limit_bytes=56 * 1024 * 1024),
        cost_estimate=pl.CostEstimate(flops=heads * 1_000_000, bytes_accessed=1, transcendentals=0),
        name="attention_grads",
    )(*operands)


def finish_kernel(n_chunks, paired, chained, start, flag_ref, *refs):
    dk_ref, dv_ref = refs[-2:]
    per_chunk = (len(refs) - 2 - (2 if chained else 0)) // n_chunks
    w = HEAD_WIDTH
    at = start
    for i in range(n_chunks):
        own_ref, *term_refs = refs[i * per_chunk : (i + 1) * per_chunk]
        for h in range(own_ref.shape[1] // (2 * w)):
            cols = slice(2 * h * w, 2 * (h + 1) * w)
            total = own_ref[:, cols]
            for t, ref in enumerate(term_refs):
                term = ref[:, cols].astype(jnp.float32)
                if paired and t == 1:
                    term = jnp.where(flag_ref[0, 0] == 1, 0.0, term)
                total = total + term
            dk_ref[:, at : at + w] = total[:, :w].astype(dk_ref.dtype)
            dv_ref[:, at : at + w] = total[:, w:].astype(dv_ref.dtype)
            at += w


def finished(flag, paired, parts, first, shape, before):
    rows = shape[0]
    w = HEAD_WIDTH
    scalars = pl.BlockSpec(memory_space=pltpu.SMEM)
    step = min(rows, BLOCK)
    if before is None:
        grid = (rows // step,)
        arrays = [x for part in parts for x in part]
        in_specs = [pl.BlockSpec((step, x.shape[1]), lambda r: (r, 0)) for x in arrays]
        out_spec = pl.BlockSpec((step, shape[1]), lambda r: (r, 0))
        aliases = {}
        start = first * w
    else:
        arrays = list(parts[0])
        grid = (arrays[0].shape[1] // (2 * w),)
        in_specs = [pl.BlockSpec((rows, 2 * w), lambda h: (0, h))] * len(arrays)
        out_spec = pl.BlockSpec((rows, w), lambda h: (0, first + h))
        aliases = {len(arrays) + 1: 0, len(arrays) + 2: 1}
        arrays += list(before)
        in_specs += [pl.BlockSpec(memory_space=pl.ANY)] * 2
        start = 0
    return pl.pallas_call(
        functools.partial(finish_kernel, len(parts), paired, before is not None, start),
        out_shape=[jax.ShapeDtypeStruct(shape, jnp.bfloat16)] * 2,
        grid=grid,
        in_specs=[scalars] + in_specs,
        out_specs=[out_spec] * 2,
        input_output_aliases=aliases,
        compiler_params=pltpu.CompilerParams(vmem_limit_bytes=48 * 1024 * 1024),
        cost_estimate=pl.CostEstimate(flops=1_000_000, bytes_accessed=1, transcendentals=0),
        name="sum_key_value_grads",
    )(flag, *arrays)


def chunk_heads(kv_heads):
    total = sum(CHUNK_SHARES)
    if kv_heads % total:
        return [kv_heads]
    return [share * kv_heads // total for share in CHUNK_SHARES]


def on_device(query, key, value, out_grad, block_mask):
    rows = query.shape[0]
    kv_heads = key.shape[1] // HEAD_WIDTH
    n_pieces = WINDOW // rows
    n_head = lax.axis_size("head")
    device = lax.axis_index("ctx") * n_head + lax.axis_index("head")
    first_block = device * (rows // BLOCK)
    own_rows = lax.dynamic_slice_in_dim(block_mask, first_block, rows // BLOCK, 0)
    block = first_block + lax.broadcasted_iota(jnp.int32, own_rows.shape, 0)
    offset = lax.broadcasted_iota(jnp.int32, own_rows.shape, 1)
    usable = (own_rows > 0) & (block >= offset)
    bias = jnp.where(usable, 0.0, -jnp.inf).astype(jnp.float32)
    paired = n_pieces == 2 and n_head % 2 == 0
    flag = lax.rem(device, 2).astype(jnp.int32).reshape(1, 1)
    bf16 = jnp.bfloat16
    f32 = jnp.float32

    counts = chunk_heads(kv_heads)
    n_chunks = len(counts)
    firsts = [sum(counts[:i]) for i in range(n_chunks)]
    packs = packed(key, value, counts)
    if paired:
        far = [moved(x, 2) for x in packs]
    else:
        far = [[moved(x, j) for j in range(n_pieces, 0, -1)] for x in packs]

    def offer(i):
        return jnp.where(flag[0, 0] == 1, far[i], packs[i])

    def settle(i):
        odd = flag[0, 0] == 1
        d_far, from_pair = waiting[i]
        for_far = d_far.astype(f32) + jnp.where(odd, from_pair, 0).astype(f32)
        for_far = for_far.astype(bf16)
        terms.append([moved(for_far, -2), from_pair])
        return for_far

    dq = None
    owns, terms, waiting, offers, nears = [], [], [], [], []
    for i in range(n_chunks):
        after = []
        if paired:
            for j in range(len(offers), min(i + 2, n_chunks)):
                offers.append(offer(j))
                nears.append(swapped(offers[j]))
                after.append(offers[j])
            if i >= 2:
                after.append(settle(i - 2))
            if i >= 3:
                after.append(terms[i - 3][0])
        pieces = [far[i], nears[i]] if paired else far[i]
        dq, flag, own, *d_pieces = attention(
            flag, bias, query, out_grad, key, value, pieces, firsts[i], counts[i], dq, after
        )
        owns.append(own)
        if paired:
            waiting.append([d_pieces[0], swapped(d_pieces[1])])
        else:
            terms.append([moved(x, j - n_pieces) for j, x in enumerate(d_pieces)])
    if paired:
        for i in range(len(terms), n_chunks):
            settle(i)
    parts = [[own, *term] for own, term in zip(owns, terms)]
    early = max(1, n_chunks - 2)
    grads = finished(flag, paired, parts[:early], 0, key.shape, None)
    for i in range(early, n_chunks):
        grads = finished(flag, paired, parts[i : i + 1], firsts[i], key.shape, grads)
    return (dq, grads[0], grads[1])


def solution(mesh):
    split = P(("ctx", "head"), None)
    return jax.shard_map(
        on_device,
        mesh=mesh,
        in_specs=(split, split, split, split, P()),
        out_specs=(split, split, split),
        check_vma=False,
    )
```

```python
import functools
import math

import jax
import jax.numpy as jnp
from jax import lax
from jax.experimental import pallas as pl
from jax.experimental.pallas import tpu as pltpu
from jax.sharding import PartitionSpec as P

HEAD_WIDTH = 128
WINDOW = 1024
BLOCK = 128
PRE_SCALE = 168.0 ** (-0.5)
LOG2_SCALE = PRE_SCALE * math.log2(math.e)
AXES = ("ctx", "head")
CHUNK_SHARES = (4, 4, 4, 2, 2)
HEADS_PER_STEP = 2
ORDER = ((2, 0, 0), (3, 0, 0), (5, 1, 0), (5, 2, 1), (5, 4, 3))
NT = (((1,), (1,)), ((), ()))
NN = (((1,), (0,)), ((), ()))


def moved(block, distance):
    n = lax.axis_size(AXES[0]) * lax.axis_size(AXES[1])
    route = [(i, i + distance) for i in range(n) if 0 <= i + distance < n]
    return lax.ppermute(block, AXES, route)


def swapped(block):
    n = lax.axis_size(AXES[0]) * lax.axis_size(AXES[1])
    return lax.ppermute(block, AXES, [(i, i ^ 1) for i in range(n)])


def pack_kernel(counts, k_ref, v_ref, *out_refs):
    w = HEAD_WIDTH
    at = 0
    for heads, out_ref in zip(counts, out_refs):
        for h in range(heads):
            source = slice((at + h) * w, (at + h + 1) * w)
            out_ref[:, 2 * h * w : (2 * h + 1) * w] = k_ref[:, source]
            out_ref[:, (2 * h + 1) * w : (2 * h + 2) * w] = v_ref[:, source]
        at += heads


def packed(key, value, counts):
    rows, width = key.shape
    step = min(rows, BLOCK)
    spec = pl.BlockSpec((step, width), lambda r: (r, 0))
    widths = [2 * HEAD_WIDTH * heads for heads in counts]
    return pl.pallas_call(
        functools.partial(pack_kernel, counts),
        out_shape=[jax.ShapeDtypeStruct((rows, x), key.dtype) for x in widths],
        grid=(rows // step,),
        in_specs=[spec, spec],
        out_specs=[pl.BlockSpec((step, x), lambda r: (r, 0)) for x in widths],
        name="pack_key_value",
    )(key, value)


def dot(a, b, dims):
    return lax.dot_general(a, b, dims, preferred_element_type=jnp.float32)


def attention_kernel(n_pieces, per_group, per_step, n_extra, *refs):
    flag_ref, bias_ref, q_ref, g_ref, k_ref, v_ref = refs[:6]
    piece_refs = refs[6 : 6 + n_pieces]
    rest = refs[6 + n_pieces + n_extra :]
    dq_ref, flag_out_ref, down_ref = rest[:3]
    dpiece_refs = rest[3 : 3 + n_pieces]
    k_ext, v_ext, k_turned, q_all, g_all, q_low, g_low, p_all, ds_all = rest[3 + n_pieces :]
    flag_out_ref[0, 0] = flag_ref[0, 0]
    rows = q_ref.shape[0]
    tiles = rows // BLOCK
    lead = n_pieces * rows
    wide = per_group * BLOCK
    span = WINDOW + BLOCK
    n_off = span // BLOCK
    w = HEAD_WIDTH
    bf16 = jnp.bfloat16

    for s in range(per_step):
        for i, piece in enumerate(piece_refs):
            k_ext[s, i * rows : (i + 1) * rows, :] = piece[:, 2 * s * w : (2 * s + 1) * w]
            v_ext[s, i * rows : (i + 1) * rows, :] = piece[:, (2 * s + 1) * w : (2 * s + 2) * w]
        k_ext[s, lead:, :] = k_ref[:, s * w : (s + 1) * w]
        v_ext[s, lead:, :] = v_ref[:, s * w : (s + 1) * w]
        k_turned[s] = k_ext[s].T
        for b in range(tiles):
            for r in range(per_group):
                at = b * wide + r * BLOCK
                source = (
                    slice(b * BLOCK, (b + 1) * BLOCK),
                    slice((s * per_group + r) * w, (s * per_group + r + 1) * w),
                )
                q_all[s, at : at + BLOCK, :] = q_ref[source]
                g_all[s, at : at + BLOCK, :] = g_ref[source]

    k_index = lax.broadcasted_iota(jnp.int32, (BLOCK, wide), 0)
    q_index = lax.rem(lax.broadcasted_iota(jnp.int32, (BLOCK, wide), 1), BLOCK)
    lower = k_index <= q_index
    group = 3 * BLOCK if n_off % 3 == 0 else BLOCK
    units = [(s, b) for s in range(per_step) for b in range(tiles)]

    def group_steps(u, key_ref, query_ref, parts):
        s, b = units[u]

        def one(start):
            top = b * BLOCK + start
            out = dot(key_ref[s, top : top + group, :], query_ref[s, b * wide : (b + 1) * wide, :], NT)
            parts.extend(out[i * BLOCK : (i + 1) * BLOCK] for i in range(group // BLOCK))

        return [functools.partial(one, start) for start in range(0, span, group)]

    def folded(x, op):
        return op(x.reshape(BLOCK // 8, 8, wide), axis=0)

    def edge_first(parts, bias0):
        first = parts[0] if bias0 is None else parts[0] + bias0
        return [jnp.where(lower, parts[-1], first)] + parts[1:-1]

    def key_steps(s):
        n_key = (lead + rows) // BLOCK
        steps = []

        def one(j, end, low, high):
            here = slice(j * BLOCK, end * BLOCK)
            cols = slice(low * wide, (high + 1) * wide)
            dv = dot(p_all[s, here, cols], g_low[s, cols, :], NN)
            dk = dot(ds_all[s, here, cols], q_low[s, cols, :], NN) * PRE_SCALE
            for i in range(j, end):
                target = down_ref if i * BLOCK >= lead else dpiece_refs[i * BLOCK // rows]
                there = slice(i * BLOCK % rows, i * BLOCK % rows + BLOCK)
                part = slice((i - j) * BLOCK, (i - j + 1) * BLOCK)
                target[there, 2 * s * w : (2 * s + 1) * w] = dk[part].astype(target.dtype)
                target[there, (2 * s + 1) * w : (2 * s + 2) * w] = dv[part].astype(target.dtype)

        j = 0
        while j < n_key:
            use = max(0, j - n_off + 1), min(tiles - 1, j)
            end = j + 1
            while end < n_key and (max(0, end - n_off + 1), min(tiles - 1, end)) == use:
                end += 1
            steps.append(functools.partial(one, j, end, *use))
            j = end
        return steps

    pending = []
    scores = [[] for _ in units]
    d_probs = [[] for _ in units]
    for step in group_steps(0, k_ext, q_all, scores[0]) + group_steps(0, v_ext, g_all, d_probs[0]):
        step()

    for u, (s, b) in enumerate(units):
        top = b * BLOCK
        cols = slice(b * wide, (b + 1) * wide)
        ahead = group_steps(u + 1, k_ext, q_all, scores[u + 1]) if u + 1 < len(units) else []
        later = group_steps(u + 1, v_ext, g_all, d_probs[u + 1]) if u + 1 < len(units) else []
        bias = [bias_ref[b, n_off - 1 - i] for i in range(n_off - 1)]
        parts = edge_first(scores[u], bias[0])
        shifts = [None] + bias[1:]
        best = folded(parts[0], jnp.max)
        for part, shift in zip(parts[1:], shifts[1:]):
            best = jnp.maximum(best, folded(part, jnp.max) + shift)
        best = jnp.max(best, axis=0, keepdims=True) * LOG2_SCALE
        d_parts = edge_first(d_probs[u], None)
        total = jnp.zeros((8, wide), jnp.float32)
        moment = jnp.zeros((8, wide), jnp.float32)
        weights = []
        for i, (part, d_part, shift) in enumerate(zip(parts, d_parts, shifts)):
            if i % 3 == 0 and ahead:
                ahead.pop(0)()
            if i % 3 == 1 and pending:
                pending.pop(0)()
            x = jnp.exp2(part * LOG2_SCALE - (best if shift is None else best - shift))
            weights.append(x)
            total = total + folded(x, jnp.sum)
            moment = moment + folded(x * d_part, jnp.sum)
            if i == 0:
                p_all[s, top : top + BLOCK, cols] = jnp.where(lower, 0.0, x).astype(bf16)
                p_all[s, top + WINDOW : top + span, cols] = jnp.where(lower, x, 0.0).astype(bf16)
            else:
                p_all[s, top + i * BLOCK : top + (i + 1) * BLOCK, cols] = x.astype(bf16)
        for step in ahead:
            step()
        inverse = 1.0 / jnp.sum(total, axis=0, keepdims=True)
        delta = jnp.sum(moment, axis=0, keepdims=True) * inverse
        column = jnp.broadcast_to(inverse, (8, wide)).T[:, :1]
        q_low[s, cols, :] = (q_all[s, cols, :].astype(jnp.float32) * column).astype(bf16)
        g_low[s, cols, :] = (g_all[s, cols, :].astype(jnp.float32) * column).astype(bf16)
        for i, (x, d_part) in enumerate(zip(weights, d_parts)):
            if i % 3 == 0 and later:
                later.pop(0)()
            if i % 3 == 1 and pending:
                pending.pop(0)()
            d_score = x * (d_part - delta)
            if i == 0:
                ds_all[s, top : top + BLOCK, cols] = jnp.where(lower, 0.0, d_score).astype(bf16)
                ds_all[s, top + WINDOW : top + span, cols] = jnp.where(lower, d_score, 0.0).astype(
                    bf16
                )
            else:
                ds_all[s, top + i * BLOCK : top + (i + 1) * BLOCK, cols] = d_score.astype(bf16)
        for step in later:
            step()
        scores[u] = d_probs[u] = None

        def query_step(s=s, top=top, cols=cols, inverse=inverse):
            turned = dot(k_turned[s, :, top : top + span], ds_all[s, top : top + span, cols], NN)
            dq_two = (turned * (inverse * PRE_SCALE)).T
            for r in range(per_group):
                at = (s * per_group + r) * w
                dq_ref[top : top + BLOCK, at : at + w] = dq_two[
                    r * BLOCK : (r + 1) * BLOCK
                ].astype(dq_ref.dtype)

        pending.append(query_step)
        if b == tiles - 1:
            pending += key_steps(s)
    for step in pending:
        step()


def attention(flag, bias, query, out_grad, key, value, pieces, first, heads, dq_before, after):
    rows = query.shape[0]
    per_group = query.shape[1] // key.shape[1]
    n = len(pieces)
    w = HEAD_WIDTH
    per_step = next(x for x in (HEADS_PER_STEP, 1) if heads % x == 0 and first % x == 0)
    at = first // per_step
    q_spec = pl.BlockSpec((rows, per_step * per_group * w), lambda h: (0, at + h))
    k_spec = pl.BlockSpec((rows, per_step * w), lambda h: (0, at + h))
    kv_spec = pl.BlockSpec((rows, per_step * 2 * w), lambda h: (0, h))
    scalars = pl.BlockSpec(memory_space=pltpu.SMEM)
    in_specs = [scalars, scalars, q_spec, q_spec, k_spec, k_spec] + [kv_spec] * n
    operands = [flag, bias, query, out_grad, key, value, *pieces]
    aliases = {}
    if dq_before is not None:
        aliases = {len(operands): 0}
        operands.append(dq_before)
    operands += after
    n_extra = len(operands) - len(in_specs)
    in_specs += [pl.BlockSpec(memory_space=pl.ANY)] * n_extra
    kv_shape = (rows, heads * 2 * w)
    length = (n + 1) * rows
    wide = rows * per_group
    bf16 = jnp.bfloat16
    return pl.pallas_call(
        functools.partial(attention_kernel, n, per_group, per_step, n_extra),
        out_shape=[
            jax.ShapeDtypeStruct(query.shape, query.dtype),
            jax.ShapeDtypeStruct(flag.shape, flag.dtype),
            jax.ShapeDtypeStruct(kv_shape, jnp.float32),
        ]
        + [jax.ShapeDtypeStruct(kv_shape, bf16)] * n,
        grid=(heads // per_step,),
        in_specs=in_specs,
        out_specs=[q_spec, scalars] + [kv_spec] * (n + 1),
        scratch_shapes=[
            pltpu.VMEM((per_step, length, w), bf16),
            pltpu.VMEM((per_step, length, w), bf16),
            pltpu.VMEM((per_step, w, length), bf16),
            pltpu.VMEM((per_step, wide, w), bf16),
            pltpu.VMEM((per_step, wide, w), bf16),
            pltpu.VMEM((per_step, wide, w), bf16),
            pltpu.VMEM((per_step, wide, w), bf16),
            pltpu.VMEM((per_step, length, wide), bf16),
            pltpu.VMEM((per_step, length, wide), bf16),
        ],
        input_output_aliases=aliases,
        compiler_params=pltpu.CompilerParams(vmem_limit_bytes=56 * 1024 * 1024),
        cost_estimate=pl.CostEstimate(flops=heads * 6_000_000_000, bytes_accessed=1, transcendentals=0),
        name="attention_grads",
    )(*operands)


def finish_kernel(n_chunks, paired, chained, start, flag_ref, *refs):
    dk_ref, dv_ref = refs[-2:]
    per_chunk = (len(refs) - 2 - (2 if chained else 0)) // n_chunks
    w = HEAD_WIDTH
    at = start
    for i in range(n_chunks):
        own_ref, *term_refs = refs[i * per_chunk : (i + 1) * per_chunk]
        for h in range(own_ref.shape[1] // (2 * w)):
            cols = slice(2 * h * w, 2 * (h + 1) * w)
            total = own_ref[:, cols]
            for t, ref in enumerate(term_refs):
                term = ref[:, cols].astype(jnp.float32)
                if paired and t == 1:
                    term = jnp.where(flag_ref[0, 0] == 1, 0.0, term)
                total = total + term
            dk_ref[:, at : at + w] = total[:, :w].astype(dk_ref.dtype)
            dv_ref[:, at : at + w] = total[:, w:].astype(dv_ref.dtype)
            at += w


def finished(flag, paired, parts, first, shape, before):
    rows = shape[0]
    w = HEAD_WIDTH
    scalars = pl.BlockSpec(memory_space=pltpu.SMEM)
    step = min(rows, BLOCK)
    if before is None:
        grid = (rows // step,)
        arrays = [x for part in parts for x in part]
        in_specs = [pl.BlockSpec((step, x.shape[1]), lambda r: (r, 0)) for x in arrays]
        out_spec = pl.BlockSpec((step, shape[1]), lambda r: (r, 0))
        aliases = {}
        start = first * w
    else:
        arrays = list(parts[0])
        grid = (arrays[0].shape[1] // (2 * w),)
        in_specs = [pl.BlockSpec((rows, 2 * w), lambda h: (0, h))] * len(arrays)
        out_spec = pl.BlockSpec((rows, w), lambda h: (0, first + h))
        aliases = {len(arrays) + 1: 0, len(arrays) + 2: 1}
        arrays += list(before)
        in_specs += [pl.BlockSpec(memory_space=pl.ANY)] * 2
        start = 0
    return pl.pallas_call(
        functools.partial(finish_kernel, len(parts), paired, before is not None, start),
        out_shape=[jax.ShapeDtypeStruct(shape, jnp.bfloat16)] * 2,
        grid=grid,
        in_specs=[scalars] + in_specs,
        out_specs=[out_spec] * 2,
        input_output_aliases=aliases,
        compiler_params=pltpu.CompilerParams(vmem_limit_bytes=48 * 1024 * 1024),
        cost_estimate=pl.CostEstimate(flops=1_000_000, bytes_accessed=1, transcendentals=0),
        name="sum_key_value_grads",
    )(flag, *arrays)


def chunk_heads(kv_heads):
    total = sum(CHUNK_SHARES)
    if kv_heads % total:
        return [kv_heads]
    return [share * kv_heads // total for share in CHUNK_SHARES]


def on_device(query, key, value, out_grad, block_mask):
    rows = query.shape[0]
    kv_heads = key.shape[1] // HEAD_WIDTH
    n_pieces = WINDOW // rows
    n_head = lax.axis_size("head")
    device = lax.axis_index("ctx") * n_head + lax.axis_index("head")
    first_block = device * (rows // BLOCK)
    own_rows = lax.dynamic_slice_in_dim(block_mask, first_block, rows // BLOCK, 0)
    block = first_block + lax.broadcasted_iota(jnp.int32, own_rows.shape, 0)
    offset = lax.broadcasted_iota(jnp.int32, own_rows.shape, 1)
    usable = (own_rows > 0) & (block >= offset)
    bias = jnp.where(usable, 0.0, -jnp.inf).astype(jnp.float32)
    paired = n_pieces == 2 and n_head % 2 == 0
    flag = lax.rem(device, 2).astype(jnp.int32).reshape(1, 1)
    bf16 = jnp.bfloat16
    f32 = jnp.float32

    counts = chunk_heads(kv_heads)
    n_chunks = len(counts)
    firsts = [sum(counts[:i]) for i in range(n_chunks)]
    packs = packed(key, value, counts)
    if paired:
        far = [moved(x, 2) for x in packs]
    else:
        far = [[moved(x, j) for j in range(n_pieces, 0, -1)] for x in packs]

    def offer(i):
        return jnp.where(flag[0, 0] == 1, far[i], packs[i])

    def settle(i):
        odd = flag[0, 0] == 1
        d_far, from_pair = waiting[i]
        for_far = d_far.astype(f32) + jnp.where(odd, from_pair, 0).astype(f32)
        for_far = for_far.astype(bf16)
        terms.append([moved(for_far, -2), from_pair])
        return for_far

    dq = None
    owns, terms, waiting, offers, nears = [], [], [], [], []
    for i in range(n_chunks):
        after = []
        if paired:
            n_offers, n_settled, n_back = (min(x, n_chunks) for x in ORDER[min(i, len(ORDER) - 1)])
            for j in range(len(offers), max(n_offers, i + 1)):
                offers.append(offer(j))
                nears.append(swapped(offers[j]))
                after.append(offers[j])
            for j in range(len(terms), min(n_settled, i)):
                after.append(settle(j))
            after += [term[0] for term in terms[:n_back]]
        pieces = [far[i], nears[i]] if paired else far[i]
        dq, flag, own, *d_pieces = attention(
            flag, bias, query, out_grad, key, value, pieces, firsts[i], counts[i], dq, after
        )
        owns.append(own)
        if paired:
            waiting.append([d_pieces[0], swapped(d_pieces[1])])
        else:
            terms.append([moved(x, j - n_pieces) for j, x in enumerate(d_pieces)])
    if paired:
        for i in range(len(terms), n_chunks):
            settle(i)
    parts = [[own, *term] for own, term in zip(owns, terms)]
    early = max(1, n_chunks - 2)
    grads = finished(flag, paired, parts[:early], 0, key.shape, None)
    for i in range(early, n_chunks):
        grads = finished(flag, paired, parts[i : i + 1], firsts[i], key.shape, grads)
    return (dq, grads[0], grads[1])


def solution(mesh):
    split = P(("ctx", "head"), None)
    return jax.shard_map(
        on_device,
        mesh=mesh,
        in_specs=(split, split, split, split, P()),
        out_specs=(split, split, split),
        check_vma=False,
    )
```

```python
import functools
import math

import jax
import jax.numpy as jnp
from jax import lax
from jax.experimental import pallas as pl
from jax.experimental.pallas import tpu as pltpu
from jax.sharding import PartitionSpec as P

HEAD_WIDTH = 128
WINDOW = 1024
BLOCK = 128
PRE_SCALE = 168.0 ** (-0.5)
LOG2_SCALE = PRE_SCALE * math.log2(math.e)
AXES = ("ctx", "head")
CHUNK_SHARES = (4, 4, 4, 2, 2)
HEADS_PER_STEP = 2
ORDER = ((2, 0, 0), (3, 0, 0), (5, 1, 0), (5, 2, 1), (5, 3, 2))
TAIL_BACK = 3
NT = (((1,), (1,)), ((), ()))
NN = (((1,), (0,)), ((), ()))


def moved(block, distance):
    n = lax.axis_size(AXES[0]) * lax.axis_size(AXES[1])
    route = [(i, i + distance) for i in range(n) if 0 <= i + distance < n]
    return lax.ppermute(block, AXES, route)


def swapped(block):
    n = lax.axis_size(AXES[0]) * lax.axis_size(AXES[1])
    return lax.ppermute(block, AXES, [(i, i ^ 1) for i in range(n)])


def pack_kernel(counts, k_ref, v_ref, *out_refs):
    w = HEAD_WIDTH
    at = 0
    for heads, out_ref in zip(counts, out_refs):
        for h in range(heads):
            source = slice((at + h) * w, (at + h + 1) * w)
            out_ref[:, 2 * h * w : (2 * h + 1) * w] = k_ref[:, source]
            out_ref[:, (2 * h + 1) * w : (2 * h + 2) * w] = v_ref[:, source]
        at += heads


def packed(key, value, counts):
    rows, width = key.shape
    step = min(rows, BLOCK)
    spec = pl.BlockSpec((step, width), lambda r: (r, 0))
    widths = [2 * HEAD_WIDTH * heads for heads in counts]
    return pl.pallas_call(
        functools.partial(pack_kernel, counts),
        out_shape=[jax.ShapeDtypeStruct((rows, x), key.dtype) for x in widths],
        grid=(rows // step,),
        in_specs=[spec, spec],
        out_specs=[pl.BlockSpec((step, x), lambda r: (r, 0)) for x in widths],
        name="pack_key_value",
    )(key, value)


def dot(a, b, dims):
    return lax.dot_general(a, b, dims, preferred_element_type=jnp.float32)


def attention_kernel(n_pieces, per_group, per_step, n_extra, *refs):
    flag_ref, bias_ref, q_ref, g_ref, k_ref, v_ref = refs[:6]
    piece_refs = refs[6 : 6 + n_pieces]
    rest = refs[6 + n_pieces + n_extra :]
    dq_ref, flag_out_ref, down_ref = rest[:3]
    dpiece_refs = rest[3 : 3 + n_pieces]
    k_ext, v_ext, k_turned, v_turned, q_all, g_all, g_turned, q_low, g_low, p_all, ds_all = rest[
        3 + n_pieces :
    ]
    flag_out_ref[0, 0] = flag_ref[0, 0]
    rows = q_ref.shape[0]
    tiles = rows // BLOCK
    lead = n_pieces * rows
    wide = per_group * BLOCK
    span = WINDOW + BLOCK
    n_off = span // BLOCK
    w = HEAD_WIDTH
    bf16 = jnp.bfloat16

    for s in range(per_step):
        for i, piece in enumerate(piece_refs):
            k_ext[s, i * rows : (i + 1) * rows, :] = piece[:, 2 * s * w : (2 * s + 1) * w]
            v_ext[s, i * rows : (i + 1) * rows, :] = piece[:, (2 * s + 1) * w : (2 * s + 2) * w]
        k_ext[s, lead:, :] = k_ref[:, s * w : (s + 1) * w]
        v_ext[s, lead:, :] = v_ref[:, s * w : (s + 1) * w]
        k_turned[s] = k_ext[s].T
        v_turned[s] = v_ext[s].T
        for b in range(tiles):
            for r in range(per_group):
                at = b * wide + r * BLOCK
                source = (
                    slice(b * BLOCK, (b + 1) * BLOCK),
                    slice((s * per_group + r) * w, (s * per_group + r + 1) * w),
                )
                q_all[s, at : at + BLOCK, :] = q_ref[source]
                g_all[s, at : at + BLOCK, :] = g_ref[source]
        g_turned[s] = g_all[s].T

    k_index = lax.broadcasted_iota(jnp.int32, (BLOCK, wide), 0)
    q_index = lax.rem(lax.broadcasted_iota(jnp.int32, (BLOCK, wide), 1), BLOCK)
    lower = k_index <= q_index
    group = 3 * BLOCK if n_off % 3 == 0 else BLOCK
    units = [(s, b) for s in range(per_step) for b in range(tiles)]

    def group_steps(u, key_ref, query_ref, parts):
        s, b = units[u]

        def one(start):
            top = b * BLOCK + start
            out = dot(key_ref[s, top : top + group, :], query_ref[s, b * wide : (b + 1) * wide, :], NT)
            parts.extend(out[i * BLOCK : (i + 1) * BLOCK] for i in range(group // BLOCK))

        return [functools.partial(one, start) for start in range(0, span, group)]

    def folded(x, op):
        return op(x.reshape(BLOCK // 8, 8, wide), axis=0)

    def edge_first(parts, bias0):
        first = parts[0] if bias0 is None else parts[0] + bias0
        return [jnp.where(lower, parts[-1], first)] + parts[1:-1]

    def key_steps(s):
        n_key = (lead + rows) // BLOCK
        steps = []

        def one(j, end, low, high):
            here = slice(j * BLOCK, end * BLOCK)
            cols = slice(low * wide, (high + 1) * wide)
            dv = dot(p_all[s, here, cols], g_low[s, cols, :], NN)
            dk = dot(ds_all[s, here, cols], q_low[s, cols, :], NN) * PRE_SCALE
            for i in range(j, end):
                target = down_ref if i * BLOCK >= lead else dpiece_refs[i * BLOCK // rows]
                there = slice(i * BLOCK % rows, i * BLOCK % rows + BLOCK)
                part = slice((i - j) * BLOCK, (i - j + 1) * BLOCK)
                target[there, 2 * s * w : (2 * s + 1) * w] = dk[part].astype(target.dtype)
                target[there, (2 * s + 1) * w : (2 * s + 2) * w] = dv[part].astype(target.dtype)

        j = 0
        while j < n_key:
            use = max(0, j - n_off + 1), min(tiles - 1, j)
            end = j + 1
            while end < n_key and (max(0, end - n_off + 1), min(tiles - 1, end)) == use:
                end += 1
            steps.append(functools.partial(one, j, end, *use))
            j = end
        return steps

    pending = []
    scores = [[] for _ in units]
    for step in group_steps(0, k_ext, q_all, scores[0]):
        step()

    for u, (s, b) in enumerate(units):
        top = b * BLOCK
        span_rows = slice(top, top + span)
        cols = slice(b * wide, (b + 1) * wide)
        ahead = group_steps(u + 1, k_ext, q_all, scores[u + 1]) if u + 1 < len(units) else []
        bias = [bias_ref[b, n_off - 1 - i] for i in range(n_off - 1)]
        parts = edge_first(scores[u], bias[0])
        shifts = [None] + bias[1:]
        best = folded(parts[0], jnp.max)
        for part, shift in zip(parts[1:], shifts[1:]):
            best = jnp.maximum(best, folded(part, jnp.max) + shift)
        best = jnp.max(best, axis=0, keepdims=True) * LOG2_SCALE
        total = jnp.zeros((8, wide), jnp.float32)
        for i, (part, shift) in enumerate(zip(parts, shifts)):
            if i % 3 == 0 and ahead:
                ahead.pop(0)()
            if i % 3 == 1 and pending:
                pending.pop(0)()
            x = jnp.exp2(part * LOG2_SCALE - (best if shift is None else best - shift))
            total = total + folded(x, jnp.sum)
            if i == 0:
                edge = x
                p_all[s, top : top + BLOCK, cols] = jnp.where(lower, 0.0, x).astype(bf16)
                p_all[s, top + WINDOW : top + span, cols] = jnp.where(lower, x, 0.0).astype(bf16)
            else:
                p_all[s, top + i * BLOCK : top + (i + 1) * BLOCK, cols] = x.astype(bf16)
        for step in ahead:
            step()
        scores[u] = None
        attended = dot(v_turned[s, :, span_rows], p_all[s, span_rows, cols], NN)
        d_parts = []
        for step in group_steps(u, v_ext, g_all, d_parts):
            step()
        d_parts = edge_first(d_parts, None)
        inverse = 1.0 / jnp.sum(total, axis=0, keepdims=True)
        delta = jnp.sum(g_turned[s, :, cols].astype(jnp.float32) * attended, axis=0, keepdims=True)
        delta = delta * inverse
        column = jnp.broadcast_to(inverse, (8, wide)).T[:, :1]
        q_low[s, cols, :] = (q_all[s, cols, :].astype(jnp.float32) * column).astype(bf16)
        g_low[s, cols, :] = (g_all[s, cols, :].astype(jnp.float32) * column).astype(bf16)
        for i, d_part in enumerate(d_parts):
            if i % 3 == 1 and pending:
                pending.pop(0)()
            if i == 0:
                d_score = edge * (d_part - delta)
                ds_all[s, top : top + BLOCK, cols] = jnp.where(lower, 0.0, d_score).astype(bf16)
                ds_all[s, top + WINDOW : top + span, cols] = jnp.where(lower, d_score, 0.0).astype(
                    bf16
                )
            else:
                here = slice(top + i * BLOCK, top + (i + 1) * BLOCK)
                x = p_all[s, here, cols].astype(jnp.float32)
                ds_all[s, here, cols] = (x * (d_part - delta)).astype(bf16)

        def query_step(s=s, top=top, cols=cols, inverse=inverse):
            turned = dot(k_turned[s, :, top : top + span], ds_all[s, top : top + span, cols], NN)
            dq_two = (turned * (inverse * PRE_SCALE)).T
            for r in range(per_group):
                at = (s * per_group + r) * w
                dq_ref[top : top + BLOCK, at : at + w] = dq_two[
                    r * BLOCK : (r + 1) * BLOCK
                ].astype(dq_ref.dtype)

        pending.append(query_step)
        if b == tiles - 1:
            pending += key_steps(s)
    for step in pending:
        step()


def attention(flag, bias, query, out_grad, key, value, pieces, first, heads, dq_before, after):
    rows = query.shape[0]
    per_group = query.shape[1] // key.shape[1]
    n = len(pieces)
    w = HEAD_WIDTH
    per_step = next(x for x in (HEADS_PER_STEP, 1) if heads % x == 0 and first % x == 0)
    at = first // per_step
    q_spec = pl.BlockSpec((rows, per_step * per_group * w), lambda h: (0, at + h))
    k_spec = pl.BlockSpec((rows, per_step * w), lambda h: (0, at + h))
    kv_spec = pl.BlockSpec((rows, per_step * 2 * w), lambda h: (0, h))
    scalars = pl.BlockSpec(memory_space=pltpu.SMEM)
    in_specs = [scalars, scalars, q_spec, q_spec, k_spec, k_spec] + [kv_spec] * n
    operands = [flag, bias, query, out_grad, key, value, *pieces]
    aliases = {}
    if dq_before is not None:
        aliases = {len(operands): 0}
        operands.append(dq_before)
    operands += after
    n_extra = len(operands) - len(in_specs)
    in_specs += [pl.BlockSpec(memory_space=pl.ANY)] * n_extra
    kv_shape = (rows, heads * 2 * w)
    length = (n + 1) * rows
    wide = rows * per_group
    bf16 = jnp.bfloat16
    return pl.pallas_call(
        functools.partial(attention_kernel, n, per_group, per_step, n_extra),
        out_shape=[
            jax.ShapeDtypeStruct(query.shape, query.dtype),
            jax.ShapeDtypeStruct(flag.shape, flag.dtype),
            jax.ShapeDtypeStruct(kv_shape, jnp.float32),
        ]
        + [jax.ShapeDtypeStruct(kv_shape, bf16)] * n,
        grid=(heads // per_step,),
        in_specs=in_specs,
        out_specs=[q_spec, scalars] + [kv_spec] * (n + 1),
        scratch_shapes=[
            pltpu.VMEM((per_step, length, w), bf16),
            pltpu.VMEM((per_step, length, w), bf16),
            pltpu.VMEM((per_step, w, length), bf16),
            pltpu.VMEM((per_step, w, length), bf16),
            pltpu.VMEM((per_step, wide, w), bf16),
            pltpu.VMEM((per_step, wide, w), bf16),
            pltpu.VMEM((per_step, w, wide), bf16),
            pltpu.VMEM((per_step, wide, w), bf16),
            pltpu.VMEM((per_step, wide, w), bf16),
            pltpu.VMEM((per_step, length, wide), bf16),
            pltpu.VMEM((per_step, length, wide), bf16),
        ],
        input_output_aliases=aliases,
        compiler_params=pltpu.CompilerParams(vmem_limit_bytes=56 * 1024 * 1024),
        cost_estimate=pl.CostEstimate(flops=heads * 6_000_000_000, bytes_accessed=1, transcendentals=0),
        name="attention_grads",
    )(*operands)


def finish_kernel(n_chunks, paired, chained, start, flag_ref, *refs):
    dk_ref, dv_ref = refs[-2:]
    per_chunk = (len(refs) - 2 - (2 if chained else 0)) // n_chunks
    w = HEAD_WIDTH
    at = start
    for i in range(n_chunks):
        own_ref, *term_refs = refs[i * per_chunk : (i + 1) * per_chunk]
        for h in range(own_ref.shape[1] // (2 * w)):
            cols = slice(2 * h * w, 2 * (h + 1) * w)
            total = own_ref[:, cols]
            for t, ref in enumerate(term_refs):
                term = ref[:, cols].astype(jnp.float32)
                if paired and t == 1:
                    term = jnp.where(flag_ref[0, 0] == 1, 0.0, term)
                total = total + term
            dk_ref[:, at : at + w] = total[:, :w].astype(dk_ref.dtype)
            dv_ref[:, at : at + w] = total[:, w:].astype(dv_ref.dtype)
            at += w


def finished(flag, paired, parts, first, shape, before):
    rows = shape[0]
    w = HEAD_WIDTH
    scalars = pl.BlockSpec(memory_space=pltpu.SMEM)
    step = min(rows, BLOCK)
    if before is None:
        grid = (rows // step,)
        arrays = [x for part in parts for x in part]
        in_specs = [pl.BlockSpec((step, x.shape[1]), lambda r: (r, 0)) for x in arrays]
        out_spec = pl.BlockSpec((step, shape[1]), lambda r: (r, 0))
        aliases = {}
        start = first * w
    else:
        arrays = list(parts[0])
        grid = (arrays[0].shape[1] // (2 * w),)
        in_specs = [pl.BlockSpec((rows, 2 * w), lambda h: (0, h))] * len(arrays)
        out_spec = pl.BlockSpec((rows, w), lambda h: (0, first + h))
        aliases = {len(arrays) + 1: 0, len(arrays) + 2: 1}
        arrays += list(before)
        in_specs += [pl.BlockSpec(memory_space=pl.ANY)] * 2
        start = 0
    return pl.pallas_call(
        functools.partial(finish_kernel, len(parts), paired, before is not None, start),
        out_shape=[jax.ShapeDtypeStruct(shape, jnp.bfloat16)] * 2,
        grid=grid,
        in_specs=[scalars] + in_specs,
        out_specs=[out_spec] * 2,
        input_output_aliases=aliases,
        compiler_params=pltpu.CompilerParams(vmem_limit_bytes=48 * 1024 * 1024),
        cost_estimate=pl.CostEstimate(flops=1_000_000, bytes_accessed=1, transcendentals=0),
        name="sum_key_value_grads",
    )(flag, *arrays)


def gate_kernel(flag_ref, *refs):
    refs[-1][0, 0] = flag_ref[0, 0]


def gated(flag, after):
    scalars = pl.BlockSpec(memory_space=pltpu.SMEM)
    return pl.pallas_call(
        gate_kernel,
        out_shape=jax.ShapeDtypeStruct(flag.shape, flag.dtype),
        in_specs=[scalars] + [pl.BlockSpec(memory_space=pl.ANY)] * len(after),
        out_specs=scalars,
        name="wait_for_returns",
    )(flag, *after)


def chunk_heads(kv_heads):
    total = sum(CHUNK_SHARES)
    if kv_heads % total:
        return [kv_heads]
    return [share * kv_heads // total for share in CHUNK_SHARES]


def on_device(query, key, value, out_grad, block_mask):
    rows = query.shape[0]
    kv_heads = key.shape[1] // HEAD_WIDTH
    n_pieces = WINDOW // rows
    n_head = lax.axis_size("head")
    device = lax.axis_index("ctx") * n_head + lax.axis_index("head")
    first_block = device * (rows // BLOCK)
    own_rows = lax.dynamic_slice_in_dim(block_mask, first_block, rows // BLOCK, 0)
    block = first_block + lax.broadcasted_iota(jnp.int32, own_rows.shape, 0)
    offset = lax.broadcasted_iota(jnp.int32, own_rows.shape, 1)
    usable = (own_rows > 0) & (block >= offset)
    bias = jnp.where(usable, 0.0, -jnp.inf).astype(jnp.float32)
    paired = n_pieces == 2 and n_head % 2 == 0
    flag = lax.rem(device, 2).astype(jnp.int32).reshape(1, 1)
    bf16 = jnp.bfloat16
    f32 = jnp.float32

    counts = chunk_heads(kv_heads)
    n_chunks = len(counts)
    firsts = [sum(counts[:i]) for i in range(n_chunks)]
    packs = packed(key, value, counts)
    if paired:
        far = [moved(x, 2) for x in packs]
    else:
        far = [[moved(x, j) for j in range(n_pieces, 0, -1)] for x in packs]

    def offer(i):
        return jnp.where(flag[0, 0] == 1, far[i], packs[i])

    def settle(i):
        odd = flag[0, 0] == 1
        d_far, from_pair = waiting[i]
        for_far = d_far.astype(f32) + jnp.where(odd, from_pair, 0).astype(f32)
        for_far = for_far.astype(bf16)
        terms.append([moved(for_far, -2), from_pair])
        return for_far

    dq = None
    owns, terms, waiting, offers, nears = [], [], [], [], []
    for i in range(n_chunks):
        after = []
        if paired:
            n_offers, n_settled, n_back = (min(x, n_chunks) for x in ORDER[min(i, len(ORDER) - 1)])
            for j in range(len(offers), max(n_offers, i + 1)):
                offers.append(offer(j))
                nears.append(swapped(offers[j]))
                after.append(offers[j])
            for j in range(len(terms), min(n_settled, i)):
                after.append(settle(j))
            after += [term[0] for term in terms[:n_back]]
        pieces = [far[i], nears[i]] if paired else far[i]
        dq, flag, own, *d_pieces = attention(
            flag, bias, query, out_grad, key, value, pieces, firsts[i], counts[i], dq, after
        )
        owns.append(own)
        if paired:
            waiting.append([d_pieces[0], swapped(d_pieces[1])])
        else:
            terms.append([moved(x, j - n_pieces) for j, x in enumerate(d_pieces)])
    if paired:
        if TAIL_BACK:
            flag = gated(flag, [term[0] for term in terms[:TAIL_BACK]])
        for i in range(len(terms), n_chunks):
            settle(i)
    parts = [[own, *term] for own, term in zip(owns, terms)]
    early = max(1, n_chunks - 2)
    grads = finished(flag, paired, parts[:early], 0, key.shape, None)
    for i in range(early, n_chunks):
        grads = finished(flag, paired, parts[i : i + 1], firsts[i], key.shape, grads)
    return (dq, grads[0], grads[1])


def solution(mesh):
    split = P(("ctx", "head"), None)
    return jax.shard_map(
        on_device,
        mesh=mesh,
        in_specs=(split, split, split, split, P()),
        out_specs=(split, split, split),
        check_vma=False,
    )
```

```python
import functools
import math

import jax
import jax.numpy as jnp
from jax import lax
from jax.experimental import pallas as pl
from jax.experimental.pallas import tpu as pltpu
from jax.sharding import PartitionSpec as P

HEAD_WIDTH = 128
WINDOW = 1024
BLOCK = 128
PRE_SCALE = 168.0 ** (-0.5)
LOG2_SCALE = PRE_SCALE * math.log2(math.e)
AXES = ("ctx", "head")
CHUNK_SHARES = (4, 4, 4, 2, 2)
HEADS_PER_STEP = 2
ORDER = ((2, 0, 0), (3, 0, 0), (5, 1, 0), (5, 2, 1), (5, 3, 2))
TAIL_BACK = 3
NT = (((1,), (1,)), ((), ()))
NN = (((1,), (0,)), ((), ()))


def moved(block, distance):
    n = lax.axis_size(AXES[0]) * lax.axis_size(AXES[1])
    route = [(i, i + distance) for i in range(n) if 0 <= i + distance < n]
    return lax.ppermute(block, AXES, route)


def swapped(block):
    n = lax.axis_size(AXES[0]) * lax.axis_size(AXES[1])
    return lax.ppermute(block, AXES, [(i, i ^ 1) for i in range(n)])


def pack_kernel(first, counts, k_ref, v_ref, *refs):
    w = HEAD_WIDTH
    at = first
    for heads, out_ref in zip(counts, refs[-len(counts) :]):
        for h in range(heads):
            source = slice((at + h) * w, (at + h + 1) * w)
            out_ref[:, 2 * h * w : (2 * h + 1) * w] = k_ref[:, source]
            out_ref[:, (2 * h + 1) * w : (2 * h + 2) * w] = v_ref[:, source]
        at += heads


def packed(key, value, first, counts, after):
    rows = key.shape[0]
    step = min(rows, BLOCK)
    spec = pl.BlockSpec((step, (first + sum(counts)) * HEAD_WIDTH), lambda r: (r, 0))
    widths = [2 * HEAD_WIDTH * heads for heads in counts]
    return pl.pallas_call(
        functools.partial(pack_kernel, first, counts),
        out_shape=[jax.ShapeDtypeStruct((rows, x), key.dtype) for x in widths],
        grid=(rows // step,),
        in_specs=[spec, spec] + [pl.BlockSpec(memory_space=pl.ANY)] * len(after),
        out_specs=[pl.BlockSpec((step, x), lambda r: (r, 0)) for x in widths],
        name="pack_key_value",
    )(key, value, *after)


def dot(a, b, dims):
    return lax.dot_general(a, b, dims, preferred_element_type=jnp.float32)


def attention_kernel(n_pieces, per_group, per_step, n_extra, *refs):
    flag_ref, bias_ref, q_ref, g_ref, k_ref, v_ref = refs[:6]
    piece_refs = refs[6 : 6 + n_pieces]
    rest = refs[6 + n_pieces + n_extra :]
    dq_ref, flag_out_ref, down_ref = rest[:3]
    dpiece_refs = rest[3 : 3 + n_pieces]
    k_ext, v_ext, k_turned, q_all, g_all, q_low, g_low, p_all, ds_all = rest[3 + n_pieces :]
    flag_out_ref[0, 0] = flag_ref[0, 0]
    rows = q_ref.shape[0]
    tiles = rows // BLOCK
    lead = n_pieces * rows
    wide = per_group * BLOCK
    span = WINDOW + BLOCK
    n_off = span // BLOCK
    w = HEAD_WIDTH
    bf16 = jnp.bfloat16

    for s in range(per_step):
        for i, piece in enumerate(piece_refs):
            k_ext[s, i * rows : (i + 1) * rows, :] = piece[:, 2 * s * w : (2 * s + 1) * w]
            v_ext[s, i * rows : (i + 1) * rows, :] = piece[:, (2 * s + 1) * w : (2 * s + 2) * w]
        k_ext[s, lead:, :] = k_ref[:, s * w : (s + 1) * w]
        v_ext[s, lead:, :] = v_ref[:, s * w : (s + 1) * w]
        k_turned[s] = k_ext[s].T
        for b in range(tiles):
            for r in range(per_group):
                at = b * wide + r * BLOCK
                source = (
                    slice(b * BLOCK, (b + 1) * BLOCK),
                    slice((s * per_group + r) * w, (s * per_group + r + 1) * w),
                )
                q_all[s, at : at + BLOCK, :] = q_ref[source]
                g_all[s, at : at + BLOCK, :] = g_ref[source]

    k_index = lax.broadcasted_iota(jnp.int32, (BLOCK, wide), 0)
    q_index = lax.rem(lax.broadcasted_iota(jnp.int32, (BLOCK, wide), 1), BLOCK)
    lower = k_index <= q_index
    group = span
    units = [(s, b) for s in range(per_step) for b in range(tiles)]

    def group_steps(u, key_ref, query_ref, parts):
        s, b = units[u]

        def one(start):
            top = b * BLOCK + start
            out = dot(key_ref[s, top : top + group, :], query_ref[s, b * wide : (b + 1) * wide, :], NT)
            parts.extend(out[i * BLOCK : (i + 1) * BLOCK] for i in range(group // BLOCK))

        return [functools.partial(one, start) for start in range(0, span, group)]

    def folded(x, op):
        return op(x.reshape(BLOCK // 8, 8, wide), axis=0)

    def edge_first(parts, bias0):
        first = parts[0] if bias0 is None else parts[0] + bias0
        return [jnp.where(lower, parts[-1], first)] + parts[1:-1]

    def key_steps(s):
        n_key = (lead + rows) // BLOCK
        steps = []

        def one(j, end, low, high):
            here = slice(j * BLOCK, end * BLOCK)
            cols = slice(low * wide, (high + 1) * wide)
            dv = dot(p_all[s, here, cols], g_low[s, cols, :], NN)
            dk = dot(ds_all[s, here, cols], q_low[s, cols, :], NN) * PRE_SCALE
            for i in range(j, end):
                target = down_ref if i * BLOCK >= lead else dpiece_refs[i * BLOCK // rows]
                there = slice(i * BLOCK % rows, i * BLOCK % rows + BLOCK)
                part = slice((i - j) * BLOCK, (i - j + 1) * BLOCK)
                target[there, 2 * s * w : (2 * s + 1) * w] = dk[part].astype(target.dtype)
                target[there, (2 * s + 1) * w : (2 * s + 2) * w] = dv[part].astype(target.dtype)

        j = 0
        while j < n_key:
            use = max(0, j - n_off + 1), min(tiles - 1, j)
            end = j + 1
            while end < n_key and (max(0, end - n_off + 1), min(tiles - 1, end)) == use:
                end += 1
            steps.append(functools.partial(one, j, end, *use))
            j = end
        return steps

    pending = []
    scores = [[] for _ in units]
    d_probs = [[] for _ in units]
    for step in group_steps(0, k_ext, q_all, scores[0]) + group_steps(0, v_ext, g_all, d_probs[0]):
        step()

    for u, (s, b) in enumerate(units):
        top = b * BLOCK
        cols = slice(b * wide, (b + 1) * wide)
        ahead = group_steps(u + 1, k_ext, q_all, scores[u + 1]) if u + 1 < len(units) else []
        later = group_steps(u + 1, v_ext, g_all, d_probs[u + 1]) if u + 1 < len(units) else []
        bias = [bias_ref[b, n_off - 1 - i] for i in range(n_off - 1)]
        parts = edge_first(scores[u], bias[0])
        shifts = [None] + bias[1:]
        best = folded(parts[0], jnp.max)
        for part, shift in zip(parts[1:], shifts[1:]):
            best = jnp.maximum(best, folded(part, jnp.max) + shift)
        best = jnp.max(best, axis=0, keepdims=True) * LOG2_SCALE
        d_parts = edge_first(d_probs[u], None)
        total = jnp.zeros((8, wide), jnp.float32)
        moment = jnp.zeros((8, wide), jnp.float32)
        weights = []
        for i, (part, d_part, shift) in enumerate(zip(parts, d_parts, shifts)):
            if i % 3 == 0 and ahead:
                ahead.pop(0)()
            if i % 3 == 1 and pending:
                pending.pop(0)()
            x = jnp.exp2(part * LOG2_SCALE - (best if shift is None else best - shift))
            weights.append(x)
            total = total + folded(x, jnp.sum)
            moment = moment + folded(x * d_part, jnp.sum)
            if i == 0:
                p_all[s, top : top + BLOCK, cols] = jnp.where(lower, 0.0, x).astype(bf16)
                p_all[s, top + WINDOW : top + span, cols] = jnp.where(lower, x, 0.0).astype(bf16)
            else:
                p_all[s, top + i * BLOCK : top + (i + 1) * BLOCK, cols] = x.astype(bf16)
        for step in ahead:
            step()
        inverse = 1.0 / jnp.sum(total, axis=0, keepdims=True)
        delta = jnp.sum(moment, axis=0, keepdims=True) * inverse
        column = jnp.broadcast_to(inverse, (8, wide)).T[:, :1]
        q_low[s, cols, :] = (q_all[s, cols, :].astype(jnp.float32) * column).astype(bf16)
        g_low[s, cols, :] = (g_all[s, cols, :].astype(jnp.float32) * column).astype(bf16)
        for i, (x, d_part) in enumerate(zip(weights, d_parts)):
            if i % 3 == 0 and later:
                later.pop(0)()
            if i % 3 == 1 and pending:
                pending.pop(0)()
            d_score = x * (d_part - delta)
            if i == 0:
                ds_all[s, top : top + BLOCK, cols] = jnp.where(lower, 0.0, d_score).astype(bf16)
                ds_all[s, top + WINDOW : top + span, cols] = jnp.where(lower, d_score, 0.0).astype(
                    bf16
                )
            else:
                ds_all[s, top + i * BLOCK : top + (i + 1) * BLOCK, cols] = d_score.astype(bf16)
        for step in later:
            step()
        scores[u] = d_probs[u] = None

        def query_step(s=s, top=top, cols=cols, inverse=inverse):
            turned = dot(k_turned[s, :, top : top + span], ds_all[s, top : top + span, cols], NN)
            dq_two = (turned * (inverse * PRE_SCALE)).T
            for r in range(per_group):
                at = (s * per_group + r) * w
                dq_ref[top : top + BLOCK, at : at + w] = dq_two[
                    r * BLOCK : (r + 1) * BLOCK
                ].astype(dq_ref.dtype)

        pending.append(query_step)
        if b == tiles - 1:
            pending += key_steps(s)
    for step in pending:
        step()


def attention(flag, bias, query, out_grad, key, value, pieces, first, heads, dq_before, after):
    rows = query.shape[0]
    per_group = query.shape[1] // key.shape[1]
    n = len(pieces)
    w = HEAD_WIDTH
    per_step = next(x for x in (HEADS_PER_STEP, 1) if heads % x == 0 and first % x == 0)
    at = first // per_step
    q_spec = pl.BlockSpec((rows, per_step * per_group * w), lambda h: (0, at + h))
    k_spec = pl.BlockSpec((rows, per_step * w), lambda h: (0, at + h))
    kv_spec = pl.BlockSpec((rows, per_step * 2 * w), lambda h: (0, h))
    scalars = pl.BlockSpec(memory_space=pltpu.SMEM)
    in_specs = [scalars, scalars, q_spec, q_spec, k_spec, k_spec] + [kv_spec] * n
    operands = [flag, bias, query, out_grad, key, value, *pieces]
    aliases = {}
    if dq_before is not None:
        aliases = {len(operands): 0}
        operands.append(dq_before)
    operands += after
    n_extra = len(operands) - len(in_specs)
    in_specs += [pl.BlockSpec(memory_space=pl.ANY)] * n_extra
    kv_shape = (rows, heads * 2 * w)
    length = (n + 1) * rows
    wide = rows * per_group
    bf16 = jnp.bfloat16
    return pl.pallas_call(
        functools.partial(attention_kernel, n, per_group, per_step, n_extra),
        out_shape=[
            jax.ShapeDtypeStruct(query.shape, query.dtype),
            jax.ShapeDtypeStruct(flag.shape, flag.dtype),
            jax.ShapeDtypeStruct(kv_shape, jnp.float32),
        ]
        + [jax.ShapeDtypeStruct(kv_shape, bf16)] * n,
        grid=(heads // per_step,),
        in_specs=in_specs,
        out_specs=[q_spec, scalars] + [kv_spec] * (n + 1),
        scratch_shapes=[
            pltpu.VMEM((per_step, length, w), bf16),
            pltpu.VMEM((per_step, length, w), bf16),
            pltpu.VMEM((per_step, w, length), bf16),
            pltpu.VMEM((per_step, wide, w), bf16),
            pltpu.VMEM((per_step, wide, w), bf16),
            pltpu.VMEM((per_step, wide, w), bf16),
            pltpu.VMEM((per_step, wide, w), bf16),
            pltpu.VMEM((per_step, length, wide), bf16),
            pltpu.VMEM((per_step, length, wide), bf16),
        ],
        input_output_aliases=aliases,
        compiler_params=pltpu.CompilerParams(vmem_limit_bytes=56 * 1024 * 1024),
        cost_estimate=pl.CostEstimate(flops=heads * 6_000_000_000, bytes_accessed=1, transcendentals=0),
        name="attention_grads",
    )(*operands)


def finish_kernel(n_chunks, paired, chained, start, flag_ref, *refs):
    dk_ref, dv_ref = refs[-2:]
    per_chunk = (len(refs) - 2 - (2 if chained else 0)) // n_chunks
    w = HEAD_WIDTH
    at = start
    for i in range(n_chunks):
        own_ref, *term_refs = refs[i * per_chunk : (i + 1) * per_chunk]
        for h in range(own_ref.shape[1] // (2 * w)):
            cols = slice(2 * h * w, 2 * (h + 1) * w)
            total = own_ref[:, cols]
            for t, ref in enumerate(term_refs):
                term = ref[:, cols].astype(jnp.float32)
                if paired and t == 1:
                    term = jnp.where(flag_ref[0, 0] == 1, 0.0, term)
                total = total + term
            dk_ref[:, at : at + w] = total[:, :w].astype(dk_ref.dtype)
            dv_ref[:, at : at + w] = total[:, w:].astype(dv_ref.dtype)
            at += w


def finished(flag, paired, parts, first, shape, before):
    rows = shape[0]
    w = HEAD_WIDTH
    scalars = pl.BlockSpec(memory_space=pltpu.SMEM)
    step = min(rows, BLOCK)
    if before is None:
        grid = (rows // step,)
        arrays = [x for part in parts for x in part]
        in_specs = [pl.BlockSpec((step, x.shape[1]), lambda r: (r, 0)) for x in arrays]
        out_spec = pl.BlockSpec((step, shape[1]), lambda r: (r, 0))
        aliases = {}
        start = first * w
    else:
        arrays = list(parts[0])
        grid = (arrays[0].shape[1] // (2 * w),)
        in_specs = [pl.BlockSpec((rows, 2 * w), lambda h: (0, h))] * len(arrays)
        out_spec = pl.BlockSpec((rows, w), lambda h: (0, first + h))
        aliases = {len(arrays) + 1: 0, len(arrays) + 2: 1}
        arrays += list(before)
        in_specs += [pl.BlockSpec(memory_space=pl.ANY)] * 2
        start = 0
    return pl.pallas_call(
        functools.partial(finish_kernel, len(parts), paired, before is not None, start),
        out_shape=[jax.ShapeDtypeStruct(shape, jnp.bfloat16)] * 2,
        grid=grid,
        in_specs=[scalars] + in_specs,
        out_specs=[out_spec] * 2,
        input_output_aliases=aliases,
        compiler_params=pltpu.CompilerParams(vmem_limit_bytes=48 * 1024 * 1024),
        cost_estimate=pl.CostEstimate(flops=1_000_000, bytes_accessed=1, transcendentals=0),
        name="sum_key_value_grads",
    )(flag, *arrays)


def gate_kernel(flag_ref, *refs):
    refs[-1][0, 0] = flag_ref[0, 0]


def gated(flag, after):
    scalars = pl.BlockSpec(memory_space=pltpu.SMEM)
    return pl.pallas_call(
        gate_kernel,
        out_shape=jax.ShapeDtypeStruct(flag.shape, flag.dtype),
        in_specs=[scalars] + [pl.BlockSpec(memory_space=pl.ANY)] * len(after),
        out_specs=scalars,
        name="wait_for_returns",
    )(flag, *after)


def chunk_heads(kv_heads):
    total = sum(CHUNK_SHARES)
    if kv_heads % total:
        return [kv_heads]
    return [share * kv_heads // total for share in CHUNK_SHARES]


def on_device(query, key, value, out_grad, block_mask):
    rows = query.shape[0]
    kv_heads = key.shape[1] // HEAD_WIDTH
    n_pieces = WINDOW // rows
    n_head = lax.axis_size("head")
    device = lax.axis_index("ctx") * n_head + lax.axis_index("head")
    first_block = device * (rows // BLOCK)
    own_rows = lax.dynamic_slice_in_dim(block_mask, first_block, rows // BLOCK, 0)
    block = first_block + lax.broadcasted_iota(jnp.int32, own_rows.shape, 0)
    offset = lax.broadcasted_iota(jnp.int32, own_rows.shape, 1)
    usable = (own_rows > 0) & (block >= offset)
    bias = jnp.where(usable, 0.0, -jnp.inf).astype(jnp.float32)
    paired = n_pieces == 2 and n_head % 2 == 0
    flag = lax.rem(device, 2).astype(jnp.int32).reshape(1, 1)
    bf16 = jnp.bfloat16
    f32 = jnp.float32

    counts = chunk_heads(kv_heads)
    n_chunks = len(counts)
    firsts = [sum(counts[:i]) for i in range(n_chunks)]
    packs = packed(key, value, 0, counts[:1], [])
    if n_chunks > 1:
        packs += packed(key, value, counts[0], counts[1:], packs)
    if paired:
        far = [moved(x, 2) for x in packs]
    else:
        far = [[moved(x, j) for j in range(n_pieces, 0, -1)] for x in packs]

    def offer(i):
        return jnp.where(flag[0, 0] == 1, far[i], packs[i])

    def settle(i):
        odd = flag[0, 0] == 1
        d_far, from_pair = waiting[i]
        for_far = d_far.astype(f32) + jnp.where(odd, from_pair, 0).astype(f32)
        for_far = for_far.astype(bf16)
        terms.append([moved(for_far, -2), from_pair])
        return for_far

    dq = None
    owns, terms, waiting, offers, nears = [], [], [], [], []
    for i in range(n_chunks):
        after = []
        if paired:
            n_offers, n_settled, n_back = (min(x, n_chunks) for x in ORDER[min(i, len(ORDER) - 1)])
            for j in range(len(offers), max(n_offers, i + 1)):
                offers.append(offer(j))
                nears.append(swapped(offers[j]))
                after.append(offers[j])
            for j in range(len(terms), min(n_settled, i)):
                after.append(settle(j))
            after += [term[0] for term in terms[:n_back]]
        pieces = [far[i], nears[i]] if paired else far[i]
        dq, flag, own, *d_pieces = attention(
            flag, bias, query, out_grad, key, value, pieces, firsts[i], counts[i], dq, after
        )
        owns.append(own)
        if paired:
            waiting.append([d_pieces[0], swapped(d_pieces[1])])
        else:
            terms.append([moved(x, j - n_pieces) for j, x in enumerate(d_pieces)])
    if paired:
        if TAIL_BACK:
            flag = gated(flag, [term[0] for term in terms[:TAIL_BACK]])
        for i in range(len(terms), n_chunks):
            settle(i)
    parts = [[own, *term] for own, term in zip(owns, terms)]
    early = max(1, n_chunks - 2)
    grads = finished(flag, paired, parts[:early], 0, key.shape, None)
    for i in range(early, n_chunks):
        grads = finished(flag, paired, parts[i : i + 1], firsts[i], key.shape, grads)
    return (dq, grads[0], grads[1])


def solution(mesh):
    split = P(("ctx", "head"), None)
    return jax.shard_map(
        on_device,
        mesh=mesh,
        in_specs=(split, split, split, split, P()),
        out_specs=(split, split, split),
        check_vma=False,
    )
```

```python
import functools
import math

import jax
import jax.numpy as jnp
from jax import lax
from jax.experimental import pallas as pl
from jax.experimental.pallas import tpu as pltpu
from jax.sharding import PartitionSpec as P

HEAD_WIDTH = 128
WINDOW = 1024
BLOCK = 128
PRE_SCALE = 168.0 ** (-0.5)
LOG2_SCALE = PRE_SCALE * math.log2(math.e)
AXES = ("ctx", "head")
CHUNK_SHARES = (4, 4, 4, 2, 2)
HEADS_PER_STEP = 2
ORDER = ((2, 0, 0), (3, 0, 0), (4, 1, 0), (5, 2, 1), (5, 3, 2))
GATES = (-1, -1, -1, -1, 2)
NT = (((1,), (1,)), ((), ()))
NN = (((1,), (0,)), ((), ()))


def moved(block, distance):
    n = lax.axis_size(AXES[0]) * lax.axis_size(AXES[1])
    route = [(i, i + distance) for i in range(n) if 0 <= i + distance < n]
    return lax.ppermute(block, AXES, route)


def swapped(block):
    n = lax.axis_size(AXES[0]) * lax.axis_size(AXES[1])
    return lax.ppermute(block, AXES, [(i, i ^ 1) for i in range(n)])


def pack_kernel(first, counts, k_ref, v_ref, *refs):
    w = HEAD_WIDTH
    at = first
    for heads, out_ref in zip(counts, refs[-len(counts) :]):
        for h in range(heads):
            source = slice((at + h) * w, (at + h + 1) * w)
            out_ref[:, 2 * h * w : (2 * h + 1) * w] = k_ref[:, source]
            out_ref[:, (2 * h + 1) * w : (2 * h + 2) * w] = v_ref[:, source]
        at += heads


def packed(key, value, first, counts, after):
    rows = key.shape[0]
    step = min(rows, BLOCK)
    spec = pl.BlockSpec((step, (first + sum(counts)) * HEAD_WIDTH), lambda r: (r, 0))
    widths = [2 * HEAD_WIDTH * heads for heads in counts]
    return pl.pallas_call(
        functools.partial(pack_kernel, first, counts),
        out_shape=[jax.ShapeDtypeStruct((rows, x), key.dtype) for x in widths],
        grid=(rows // step,),
        in_specs=[spec, spec] + [pl.BlockSpec(memory_space=pl.ANY)] * len(after),
        out_specs=[pl.BlockSpec((step, x), lambda r: (r, 0)) for x in widths],
        name="pack_key_value",
    )(key, value, *after)


def dot(a, b, dims):
    return lax.dot_general(a, b, dims, preferred_element_type=jnp.float32)


def attention_kernel(n_pieces, per_group, per_step, n_extra, *refs):
    flag_ref, bias_ref, q_ref, g_ref, k_ref, v_ref = refs[:6]
    piece_refs = refs[6 : 6 + n_pieces]
    rest = refs[6 + n_pieces + n_extra :]
    dq_ref, flag_out_ref, down_ref = rest[:3]
    dpiece_refs = rest[3 : 3 + n_pieces]
    k_ext, v_ext, k_turned, q_all, g_all, q_low, g_low, p_all, ds_all = rest[3 + n_pieces :]
    flag_out_ref[0, 0] = flag_ref[0, 0]
    rows = q_ref.shape[0]
    tiles = rows // BLOCK
    lead = n_pieces * rows
    wide = per_group * BLOCK
    span = WINDOW + BLOCK
    n_off = span // BLOCK
    w = HEAD_WIDTH
    bf16 = jnp.bfloat16

    for s in range(per_step):
        for i, piece in enumerate(piece_refs):
            k_ext[s, i * rows : (i + 1) * rows, :] = piece[:, 2 * s * w : (2 * s + 1) * w]
            v_ext[s, i * rows : (i + 1) * rows, :] = piece[:, (2 * s + 1) * w : (2 * s + 2) * w]
        k_ext[s, lead:, :] = k_ref[:, s * w : (s + 1) * w]
        v_ext[s, lead:, :] = v_ref[:, s * w : (s + 1) * w]
        k_turned[s] = k_ext[s].T
        for b in range(tiles):
            for r in range(per_group):
                at = b * wide + r * BLOCK
                source = (
                    slice(b * BLOCK, (b + 1) * BLOCK),
                    slice((s * per_group + r) * w, (s * per_group + r + 1) * w),
                )
                q_all[s, at : at + BLOCK, :] = q_ref[source]
                g_all[s, at : at + BLOCK, :] = g_ref[source]

    k_index = lax.broadcasted_iota(jnp.int32, (BLOCK, wide), 0)
    q_index = lax.rem(lax.broadcasted_iota(jnp.int32, (BLOCK, wide), 1), BLOCK)
    lower = k_index <= q_index
    group = span
    units = [(s, b) for s in range(per_step) for b in range(tiles)]

    def group_steps(u, key_ref, query_ref, parts):
        s, b = units[u]

        def one(start):
            top = b * BLOCK + start
            out = dot(key_ref[s, top : top + group, :], query_ref[s, b * wide : (b + 1) * wide, :], NT)
            parts.extend(out[i * BLOCK : (i + 1) * BLOCK] for i in range(group // BLOCK))

        return [functools.partial(one, start) for start in range(0, span, group)]

    def folded(x, op):
        return op(x.reshape(BLOCK // 8, 8, wide), axis=0)

    def edge_first(parts, bias0):
        first = parts[0] if bias0 is None else parts[0] + bias0
        return [jnp.where(lower, parts[-1], first)] + parts[1:-1]

    def key_steps(s):
        n_key = (lead + rows) // BLOCK
        steps = []

        def one(j, end, low, high):
            here = slice(j * BLOCK, end * BLOCK)
            cols = slice(low * wide, (high + 1) * wide)
            dv = dot(p_all[s, here, cols], g_low[s, cols, :], NN)
            dk = dot(ds_all[s, here, cols], q_low[s, cols, :], NN) * PRE_SCALE
            for i in range(j, end):
                target = down_ref if i * BLOCK >= lead else dpiece_refs[i * BLOCK // rows]
                there = slice(i * BLOCK % rows, i * BLOCK % rows + BLOCK)
                part = slice((i - j) * BLOCK, (i - j + 1) * BLOCK)
                target[there, 2 * s * w : (2 * s + 1) * w] = dk[part].astype(target.dtype)
                target[there, (2 * s + 1) * w : (2 * s + 2) * w] = dv[part].astype(target.dtype)

        j = 0
        while j < n_key:
            use = max(0, j - n_off + 1), min(tiles - 1, j)
            end = j + 1
            while end < n_key and (max(0, end - n_off + 1), min(tiles - 1, end)) == use:
                end += 1
            steps.append(functools.partial(one, j, end, *use))
            j = end
        return steps

    pending = []
    scores = [[] for _ in units]
    d_probs = [[] for _ in units]
    for step in group_steps(0, k_ext, q_all, scores[0]) + group_steps(0, v_ext, g_all, d_probs[0]):
        step()

    for u, (s, b) in enumerate(units):
        top = b * BLOCK
        cols = slice(b * wide, (b + 1) * wide)
        ahead = group_steps(u + 1, k_ext, q_all, scores[u + 1]) if u + 1 < len(units) else []
        later = group_steps(u + 1, v_ext, g_all, d_probs[u + 1]) if u + 1 < len(units) else []
        bias = [bias_ref[b, n_off - 1 - i] for i in range(n_off - 1)]
        parts = edge_first(scores[u], bias[0])
        shifts = [None] + bias[1:]
        best = folded(parts[0], jnp.max)
        for part, shift in zip(parts[1:], shifts[1:]):
            best = jnp.maximum(best, folded(part, jnp.max) + shift)
        best = jnp.max(best, axis=0, keepdims=True) * LOG2_SCALE
        d_parts = edge_first(d_probs[u], None)
        total = jnp.zeros((8, wide), jnp.float32)
        moment = jnp.zeros((8, wide), jnp.float32)
        weights = []
        for i, (part, d_part, shift) in enumerate(zip(parts, d_parts, shifts)):
            if i % 3 == 0 and ahead:
                ahead.pop(0)()
            if i % 3 == 1 and pending:
                pending.pop(0)()
            x = jnp.exp2(part * LOG2_SCALE - (best if shift is None else best - shift))
            weights.append(x)
            total = total + folded(x, jnp.sum)
            moment = moment + folded(x * d_part, jnp.sum)
            if i == 0:
                p_all[s, top : top + BLOCK, cols] = jnp.where(lower, 0.0, x).astype(bf16)
                p_all[s, top + WINDOW : top + span, cols] = jnp.where(lower, x, 0.0).astype(bf16)
            else:
                p_all[s, top + i * BLOCK : top + (i + 1) * BLOCK, cols] = x.astype(bf16)
        for step in ahead:
            step()
        inverse = 1.0 / jnp.sum(total, axis=0, keepdims=True)
        delta = jnp.sum(moment, axis=0, keepdims=True) * inverse
        column = jnp.broadcast_to(inverse, (8, wide)).T[:, :1]
        q_low[s, cols, :] = (q_all[s, cols, :].astype(jnp.float32) * column).astype(bf16)
        g_low[s, cols, :] = (g_all[s, cols, :].astype(jnp.float32) * column).astype(bf16)
        for i, (x, d_part) in enumerate(zip(weights, d_parts)):
            if i % 3 == 0 and later:
                later.pop(0)()
            if i % 3 == 1 and pending:
                pending.pop(0)()
            d_score = x * (d_part - delta)
            if i == 0:
                ds_all[s, top : top + BLOCK, cols] = jnp.where(lower, 0.0, d_score).astype(bf16)
                ds_all[s, top + WINDOW : top + span, cols] = jnp.where(lower, d_score, 0.0).astype(
                    bf16
                )
            else:
                ds_all[s, top + i * BLOCK : top + (i + 1) * BLOCK, cols] = d_score.astype(bf16)
        for step in later:
            step()
        scores[u] = d_probs[u] = None

        def query_step(s=s, top=top, cols=cols, inverse=inverse):
            turned = dot(k_turned[s, :, top : top + span], ds_all[s, top : top + span, cols], NN)
            dq_two = (turned * (inverse * PRE_SCALE)).T
            for r in range(per_group):
                at = (s * per_group + r) * w
                dq_ref[top : top + BLOCK, at : at + w] = dq_two[
                    r * BLOCK : (r + 1) * BLOCK
                ].astype(dq_ref.dtype)

        pending.append(query_step)
        if b == tiles - 1:
            pending += key_steps(s)
    for step in pending:
        step()


def attention(flag, bias, query, out_grad, key, value, pieces, first, heads, dq_before, after):
    rows = query.shape[0]
    per_group = query.shape[1] // key.shape[1]
    n = len(pieces)
    w = HEAD_WIDTH
    per_step = next(x for x in (HEADS_PER_STEP, 1) if heads % x == 0 and first % x == 0)
    at = first // per_step
    q_spec = pl.BlockSpec((rows, per_step * per_group * w), lambda h: (0, at + h))
    k_spec = pl.BlockSpec((rows, per_step * w), lambda h: (0, at + h))
    kv_spec = pl.BlockSpec((rows, per_step * 2 * w), lambda h: (0, h))
    scalars = pl.BlockSpec(memory_space=pltpu.SMEM)
    in_specs = [scalars, scalars, q_spec, q_spec, k_spec, k_spec] + [kv_spec] * n
    operands = [flag, bias, query, out_grad, key, value, *pieces]
    aliases = {}
    if dq_before is not None:
        aliases = {len(operands): 0}
        operands.append(dq_before)
    operands += after
    n_extra = len(operands) - len(in_specs)
    in_specs += [pl.BlockSpec(memory_space=pl.ANY)] * n_extra
    kv_shape = (rows, heads * 2 * w)
    length = (n + 1) * rows
    wide = rows * per_group
    bf16 = jnp.bfloat16
    return pl.pallas_call(
        functools.partial(attention_kernel, n, per_group, per_step, n_extra),
        out_shape=[
            jax.ShapeDtypeStruct(query.shape, query.dtype),
            jax.ShapeDtypeStruct(flag.shape, flag.dtype),
            jax.ShapeDtypeStruct(kv_shape, jnp.float32),
        ]
        + [jax.ShapeDtypeStruct(kv_shape, bf16)] * n,
        grid=(heads // per_step,),
        in_specs=in_specs,
        out_specs=[q_spec, scalars] + [kv_spec] * (n + 1),
        scratch_shapes=[
            pltpu.VMEM((per_step, length, w), bf16),
            pltpu.VMEM((per_step, length, w), bf16),
            pltpu.VMEM((per_step, w, length), bf16),
            pltpu.VMEM((per_step, wide, w), bf16),
            pltpu.VMEM((per_step, wide, w), bf16),
            pltpu.VMEM((per_step, wide, w), bf16),
            pltpu.VMEM((per_step, wide, w), bf16),
            pltpu.VMEM((per_step, length, wide), bf16),
            pltpu.VMEM((per_step, length, wide), bf16),
        ],
        input_output_aliases=aliases,
        compiler_params=pltpu.CompilerParams(vmem_limit_bytes=56 * 1024 * 1024),
        cost_estimate=pl.CostEstimate(flops=heads * 6_000_000_000, bytes_accessed=1, transcendentals=0),
        name="attention_grads",
    )(*operands)


def finish_kernel(n_chunks, paired, chained, start, flag_ref, *refs):
    dk_ref, dv_ref = refs[-2:]
    per_chunk = (len(refs) - 2 - (2 if chained else 0)) // n_chunks
    w = HEAD_WIDTH
    at = start
    for i in range(n_chunks):
        own_ref, *term_refs = refs[i * per_chunk : (i + 1) * per_chunk]
        for h in range(own_ref.shape[1] // (2 * w)):
            cols = slice(2 * h * w, 2 * (h + 1) * w)
            total = own_ref[:, cols]
            for t, ref in enumerate(term_refs):
                term = ref[:, cols].astype(jnp.float32)
                if paired and t == 1:
                    term = jnp.where(flag_ref[0, 0] == 1, 0.0, term)
                total = total + term
            dk_ref[:, at : at + w] = total[:, :w].astype(dk_ref.dtype)
            dv_ref[:, at : at + w] = total[:, w:].astype(dv_ref.dtype)
            at += w


def finished(flag, paired, parts, first, shape, before):
    rows = shape[0]
    w = HEAD_WIDTH
    scalars = pl.BlockSpec(memory_space=pltpu.SMEM)
    step = min(rows, BLOCK)
    if before is None:
        grid = (rows // step,)
        arrays = [x for part in parts for x in part]
        in_specs = [pl.BlockSpec((step, x.shape[1]), lambda r: (r, 0)) for x in arrays]
        out_spec = pl.BlockSpec((step, shape[1]), lambda r: (r, 0))
        aliases = {}
        start = first * w
    else:
        arrays = list(parts[0])
        grid = (arrays[0].shape[1] // (2 * w),)
        in_specs = [pl.BlockSpec((rows, 2 * w), lambda h: (0, h))] * len(arrays)
        out_spec = pl.BlockSpec((rows, w), lambda h: (0, first + h))
        aliases = {len(arrays) + 1: 0, len(arrays) + 2: 1}
        arrays += list(before)
        in_specs += [pl.BlockSpec(memory_space=pl.ANY)] * 2
        start = 0
    return pl.pallas_call(
        functools.partial(finish_kernel, len(parts), paired, before is not None, start),
        out_shape=[jax.ShapeDtypeStruct(shape, jnp.bfloat16)] * 2,
        grid=grid,
        in_specs=[scalars] + in_specs,
        out_specs=[out_spec] * 2,
        input_output_aliases=aliases,
        compiler_params=pltpu.CompilerParams(vmem_limit_bytes=48 * 1024 * 1024),
        cost_estimate=pl.CostEstimate(flops=1_000_000, bytes_accessed=1, transcendentals=0),
        name="sum_key_value_grads",
    )(flag, *arrays)


def gate_kernel(flag_ref, *refs):
    refs[-1][0, 0] = flag_ref[0, 0]


def gated(flag, after):
    scalars = pl.BlockSpec(memory_space=pltpu.SMEM)
    return pl.pallas_call(
        gate_kernel,
        out_shape=jax.ShapeDtypeStruct(flag.shape, flag.dtype),
        in_specs=[scalars] + [pl.BlockSpec(memory_space=pl.ANY)] * len(after),
        out_specs=scalars,
        cost_estimate=pl.CostEstimate(flops=1, bytes_accessed=1, transcendentals=0),
        name="wait_for_returns",
    )(flag, *after)


def chunk_heads(kv_heads):
    total = sum(CHUNK_SHARES)
    if kv_heads % total:
        return [kv_heads]
    return [share * kv_heads // total for share in CHUNK_SHARES]


def on_device(query, key, value, out_grad, block_mask):
    rows = query.shape[0]
    kv_heads = key.shape[1] // HEAD_WIDTH
    n_pieces = WINDOW // rows
    n_head = lax.axis_size("head")
    device = lax.axis_index("ctx") * n_head + lax.axis_index("head")
    first_block = device * (rows // BLOCK)
    own_rows = lax.dynamic_slice_in_dim(block_mask, first_block, rows // BLOCK, 0)
    block = first_block + lax.broadcasted_iota(jnp.int32, own_rows.shape, 0)
    offset = lax.broadcasted_iota(jnp.int32, own_rows.shape, 1)
    usable = (own_rows > 0) & (block >= offset)
    bias = jnp.where(usable, 0.0, -jnp.inf).astype(jnp.float32)
    paired = n_pieces == 2 and n_head % 2 == 0
    flag = lax.rem(device, 2).astype(jnp.int32).reshape(1, 1)
    bf16 = jnp.bfloat16
    f32 = jnp.float32

    counts = chunk_heads(kv_heads)
    n_chunks = len(counts)
    firsts = [sum(counts[:i]) for i in range(n_chunks)]
    packs = packed(key, value, 0, counts[:1], [])
    if n_chunks > 1:
        packs += packed(key, value, counts[0], counts[1:], packs)
    if paired:
        far = [moved(x, 2) for x in packs]
    else:
        far = [[moved(x, j) for j in range(n_pieces, 0, -1)] for x in packs]

    def offer(i):
        return jnp.where(flag[0, 0] == 1, far[i], packs[i])

    def settle(i):
        back = GATES[min(i, len(GATES) - 1)]
        ready = gated(flag, terms[back][:1]) if 0 <= back < i else flag
        odd = ready[0, 0] == 1
        d_far, from_pair = waiting[i]
        for_far = d_far.astype(f32) + jnp.where(odd, from_pair, 0).astype(f32)
        for_far = for_far.astype(bf16)
        terms.append([moved(for_far, -2), from_pair])
        return for_far

    dq = None
    owns, terms, waiting, offers, nears = [], [], [], [], []
    for i in range(n_chunks):
        after = []
        if paired:
            n_offers, n_settled, n_back = (min(x, n_chunks) for x in ORDER[min(i, len(ORDER) - 1)])
            for j in range(len(offers), max(n_offers, i + 1)):
                offers.append(offer(j))
                nears.append(swapped(offers[j]))
                after.append(offers[j])
            for j in range(len(terms), min(n_settled, i)):
                after.append(settle(j))
            after += [term[0] for term in terms[:n_back]]
        pieces = [far[i], nears[i]] if paired else far[i]
        dq, flag, own, *d_pieces = attention(
            flag, bias, query, out_grad, key, value, pieces, firsts[i], counts[i], dq, after
        )
        owns.append(own)
        if paired:
            waiting.append([d_pieces[0], swapped(d_pieces[1])])
        else:
            terms.append([moved(x, j - n_pieces) for j, x in enumerate(d_pieces)])
    if paired:
        for i in range(len(terms), n_chunks):
            settle(i)
    parts = [[own, *term] for own, term in zip(owns, terms)]
    early = max(1, n_chunks - 2)
    grads = finished(flag, paired, parts[:early], 0, key.shape, None)
    for i in range(early, n_chunks):
        grads = finished(flag, paired, parts[i : i + 1], firsts[i], key.shape, grads)
    return (dq, grads[0], grads[1])


def solution(mesh):
    split = P(("ctx", "head"), None)
    return jax.shard_map(
        on_device,
        mesh=mesh,
        in_specs=(split, split, split, split, P()),
        out_specs=(split, split, split),
        check_vma=False,
    )
```

```python
import functools
import math

import jax
import jax.numpy as jnp
from jax import lax
from jax.experimental import pallas as pl
from jax.experimental.pallas import tpu as pltpu
from jax.sharding import PartitionSpec as P

HEAD_WIDTH = 128
WINDOW = 1024
BLOCK = 128
PRE_SCALE = 168.0 ** (-0.5)
LOG2_SCALE = PRE_SCALE * math.log2(math.e)
AXES = ("ctx", "head")
CHUNK_SHARES = (4, 4, 4, 2, 2)
HEADS_PER_STEP = 2
ORDER = ((2, 0, 0), (3, 1, 0), (4, 2, 0), (5, 3, 0), (5, 4, 0))
GATES = (-1, 0, 1, 1, 2)
ARRIVALS = ((2, 3),)
NT = (((1,), (1,)), ((), ()))
NN = (((1,), (0,)), ((), ()))


def moved(block, distance):
    n = lax.axis_size(AXES[0]) * lax.axis_size(AXES[1])
    route = [(i, i + distance) for i in range(n) if 0 <= i + distance < n]
    return lax.ppermute(block, AXES, route)


def swapped(block):
    n = lax.axis_size(AXES[0]) * lax.axis_size(AXES[1])
    return lax.ppermute(block, AXES, [(i, i ^ 1) for i in range(n)])


def pack_kernel(first, counts, k_ref, v_ref, *refs):
    w = HEAD_WIDTH
    at = first
    for heads, out_ref in zip(counts, refs[-len(counts) :]):
        for h in range(heads):
            source = slice((at + h) * w, (at + h + 1) * w)
            out_ref[:, 2 * h * w : (2 * h + 1) * w] = k_ref[:, source]
            out_ref[:, (2 * h + 1) * w : (2 * h + 2) * w] = v_ref[:, source]
        at += heads


def packed(key, value, first, counts, after):
    rows = key.shape[0]
    step = min(rows, BLOCK)
    spec = pl.BlockSpec((step, (first + sum(counts)) * HEAD_WIDTH), lambda r: (r, 0))
    widths = [2 * HEAD_WIDTH * heads for heads in counts]
    return pl.pallas_call(
        functools.partial(pack_kernel, first, counts),
        out_shape=[jax.ShapeDtypeStruct((rows, x), key.dtype) for x in widths],
        grid=(rows // step,),
        in_specs=[spec, spec] + [pl.BlockSpec(memory_space=pl.ANY)] * len(after),
        out_specs=[pl.BlockSpec((step, x), lambda r: (r, 0)) for x in widths],
        name="pack_key_value",
    )(key, value, *after)


def dot(a, b, dims):
    return lax.dot_general(a, b, dims, preferred_element_type=jnp.float32)


def attention_kernel(n_pieces, per_group, per_step, n_extra, *refs):
    flag_ref, bias_ref, q_ref, g_ref, k_ref, v_ref = refs[:6]
    piece_refs = refs[6 : 6 + n_pieces]
    rest = refs[6 + n_pieces + n_extra :]
    dq_ref, flag_out_ref, down_ref = rest[:3]
    dpiece_refs = rest[3 : 3 + n_pieces]
    k_ext, v_ext, k_turned, q_all, g_all, q_low, g_low, p_all, ds_all = rest[3 + n_pieces :]
    flag_out_ref[0, 0] = flag_ref[0, 0]
    rows = q_ref.shape[0]
    tiles = rows // BLOCK
    lead = n_pieces * rows
    wide = per_group * BLOCK
    span = WINDOW + BLOCK
    n_off = span // BLOCK
    w = HEAD_WIDTH
    bf16 = jnp.bfloat16

    for s in range(per_step):
        for i, piece in enumerate(piece_refs):
            k_ext[s, i * rows : (i + 1) * rows, :] = piece[:, 2 * s * w : (2 * s + 1) * w]
            v_ext[s, i * rows : (i + 1) * rows, :] = piece[:, (2 * s + 1) * w : (2 * s + 2) * w]
        k_ext[s, lead:, :] = k_ref[:, s * w : (s + 1) * w]
        v_ext[s, lead:, :] = v_ref[:, s * w : (s + 1) * w]
        k_turned[s] = k_ext[s].T
        for b in range(tiles):
            for r in range(per_group):
                at = b * wide + r * BLOCK
                source = (
                    slice(b * BLOCK, (b + 1) * BLOCK),
                    slice((s * per_group + r) * w, (s * per_group + r + 1) * w),
                )
                q_all[s, at : at + BLOCK, :] = q_ref[source]
                g_all[s, at : at + BLOCK, :] = g_ref[source]

    k_index = lax.broadcasted_iota(jnp.int32, (BLOCK, wide), 0)
    q_index = lax.rem(lax.broadcasted_iota(jnp.int32, (BLOCK, wide), 1), BLOCK)
    lower = k_index <= q_index
    group = span
    units = [(s, b) for s in range(per_step) for b in range(tiles)]

    def group_steps(u, key_ref, query_ref, parts):
        s, b = units[u]

        def one(start):
            top = b * BLOCK + start
            out = dot(key_ref[s, top : top + group, :], query_ref[s, b * wide : (b + 1) * wide, :], NT)
            parts.extend(out[i * BLOCK : (i + 1) * BLOCK] for i in range(group // BLOCK))

        return [functools.partial(one, start) for start in range(0, span, group)]

    def folded(x, op):
        return op(x.reshape(BLOCK // 8, 8, wide), axis=0)

    def edge_first(parts, bias0):
        first = parts[0] if bias0 is None else parts[0] + bias0
        return [jnp.where(lower, parts[-1], first)] + parts[1:-1]

    def key_steps(s):
        n_key = (lead + rows) // BLOCK
        steps = []

        def one(j, end, low, high):
            here = slice(j * BLOCK, end * BLOCK)
            cols = slice(low * wide, (high + 1) * wide)
            dv = dot(p_all[s, here, cols], g_low[s, cols, :], NN)
            dk = dot(ds_all[s, here, cols], q_low[s, cols, :], NN) * PRE_SCALE
            for i in range(j, end):
                target = down_ref if i * BLOCK >= lead else dpiece_refs[i * BLOCK // rows]
                there = slice(i * BLOCK % rows, i * BLOCK % rows + BLOCK)
                part = slice((i - j) * BLOCK, (i - j + 1) * BLOCK)
                target[there, 2 * s * w : (2 * s + 1) * w] = dk[part].astype(target.dtype)
                target[there, (2 * s + 1) * w : (2 * s + 2) * w] = dv[part].astype(target.dtype)

        j = 0
        while j < n_key:
            use = max(0, j - n_off + 1), min(tiles - 1, j)
            end = j + 1
            while end < n_key and (max(0, end - n_off + 1), min(tiles - 1, end)) == use:
                end += 1
            steps.append(functools.partial(one, j, end, *use))
            j = end
        return steps

    pending = []
    scores = [[] for _ in units]
    d_probs = [[] for _ in units]
    for step in group_steps(0, k_ext, q_all, scores[0]) + group_steps(0, v_ext, g_all, d_probs[0]):
        step()

    for u, (s, b) in enumerate(units):
        top = b * BLOCK
        cols = slice(b * wide, (b + 1) * wide)
        ahead = group_steps(u + 1, k_ext, q_all, scores[u + 1]) if u + 1 < len(units) else []
        later = group_steps(u + 1, v_ext, g_all, d_probs[u + 1]) if u + 1 < len(units) else []
        bias = [bias_ref[b, n_off - 1 - i] for i in range(n_off - 1)]
        parts = edge_first(scores[u], bias[0])
        shifts = [None] + bias[1:]
        best = folded(parts[0], jnp.max)
        for part, shift in zip(parts[1:], shifts[1:]):
            best = jnp.maximum(best, folded(part, jnp.max) + shift)
        best = jnp.max(best, axis=0, keepdims=True) * LOG2_SCALE
        d_parts = edge_first(d_probs[u], None)
        total = jnp.zeros((8, wide), jnp.float32)
        moment = jnp.zeros((8, wide), jnp.float32)
        weights = []
        for i, (part, d_part, shift) in enumerate(zip(parts, d_parts, shifts)):
            if i % 3 == 0 and ahead:
                ahead.pop(0)()
            if i % 3 == 1 and pending:
                pending.pop(0)()
            x = jnp.exp2(part * LOG2_SCALE - (best if shift is None else best - shift))
            weights.append(x)
            total = total + folded(x, jnp.sum)
            moment = moment + folded(x * d_part, jnp.sum)
            if i == 0:
                p_all[s, top : top + BLOCK, cols] = jnp.where(lower, 0.0, x).astype(bf16)
                p_all[s, top + WINDOW : top + span, cols] = jnp.where(lower, x, 0.0).astype(bf16)
            else:
                p_all[s, top + i * BLOCK : top + (i + 1) * BLOCK, cols] = x.astype(bf16)
        for step in ahead:
            step()
        inverse = 1.0 / jnp.sum(total, axis=0, keepdims=True)
        delta = jnp.sum(moment, axis=0, keepdims=True) * inverse
        column = jnp.broadcast_to(inverse, (8, wide)).T[:, :1]
        q_low[s, cols, :] = (q_all[s, cols, :].astype(jnp.float32) * column).astype(bf16)
        g_low[s, cols, :] = (g_all[s, cols, :].astype(jnp.float32) * column).astype(bf16)
        for i, (x, d_part) in enumerate(zip(weights, d_parts)):
            if i % 3 == 0 and later:
                later.pop(0)()
            if i % 3 == 1 and pending:
                pending.pop(0)()
            d_score = x * (d_part - delta)
            if i == 0:
                ds_all[s, top : top + BLOCK, cols] = jnp.where(lower, 0.0, d_score).astype(bf16)
                ds_all[s, top + WINDOW : top + span, cols] = jnp.where(lower, d_score, 0.0).astype(
                    bf16
                )
            else:
                ds_all[s, top + i * BLOCK : top + (i + 1) * BLOCK, cols] = d_score.astype(bf16)
        for step in later:
            step()
        scores[u] = d_probs[u] = None

        def query_step(s=s, top=top, cols=cols, inverse=inverse):
            turned = dot(k_turned[s, :, top : top + span], ds_all[s, top : top + span, cols], NN)
            dq_two = (turned * (inverse * PRE_SCALE)).T
            for r in range(per_group):
                at = (s * per_group + r) * w
                dq_ref[top : top + BLOCK, at : at + w] = dq_two[
                    r * BLOCK : (r + 1) * BLOCK
                ].astype(dq_ref.dtype)

        pending.append(query_step)
        if b == tiles - 1:
            pending += key_steps(s)
    for step in pending:
        step()


def attention(flag, bias, query, out_grad, key, value, pieces, first, heads, dq_before, after):
    rows = query.shape[0]
    per_group = query.shape[1] // key.shape[1]
    n = len(pieces)
    w = HEAD_WIDTH
    per_step = next(x for x in (HEADS_PER_STEP, 1) if heads % x == 0 and first % x == 0)
    at = first // per_step
    q_spec = pl.BlockSpec((rows, per_step * per_group * w), lambda h: (0, at + h))
    k_spec = pl.BlockSpec((rows, per_step * w), lambda h: (0, at + h))
    kv_spec = pl.BlockSpec((rows, per_step * 2 * w), lambda h: (0, h))
    scalars = pl.BlockSpec(memory_space=pltpu.SMEM)
    in_specs = [scalars, scalars, q_spec, q_spec, k_spec, k_spec] + [kv_spec] * n
    operands = [flag, bias, query, out_grad, key, value, *pieces]
    aliases = {}
    if dq_before is not None:
        aliases = {len(operands): 0}
        operands.append(dq_before)
    operands += after
    n_extra = len(operands) - len(in_specs)
    in_specs += [pl.BlockSpec(memory_space=pl.ANY)] * n_extra
    kv_shape = (rows, heads * 2 * w)
    length = (n + 1) * rows
    wide = rows * per_group
    bf16 = jnp.bfloat16
    return pl.pallas_call(
        functools.partial(attention_kernel, n, per_group, per_step, n_extra),
        out_shape=[
            jax.ShapeDtypeStruct(query.shape, query.dtype),
            jax.ShapeDtypeStruct(flag.shape, flag.dtype),
            jax.ShapeDtypeStruct(kv_shape, jnp.float32),
        ]
        + [jax.ShapeDtypeStruct(kv_shape, bf16)] * n,
        grid=(heads // per_step,),
        in_specs=in_specs,
        out_specs=[q_spec, scalars] + [kv_spec] * (n + 1),
        scratch_shapes=[
            pltpu.VMEM((per_step, length, w), bf16),
            pltpu.VMEM((per_step, length, w), bf16),
            pltpu.VMEM((per_step, w, length), bf16),
            pltpu.VMEM((per_step, wide, w), bf16),
            pltpu.VMEM((per_step, wide, w), bf16),
            pltpu.VMEM((per_step, wide, w), bf16),
            pltpu.VMEM((per_step, wide, w), bf16),
            pltpu.VMEM((per_step, length, wide), bf16),
            pltpu.VMEM((per_step, length, wide), bf16),
        ],
        input_output_aliases=aliases,
        compiler_params=pltpu.CompilerParams(vmem_limit_bytes=56 * 1024 * 1024),
        cost_estimate=pl.CostEstimate(flops=heads * 6_000_000_000, bytes_accessed=1, transcendentals=0),
        name="attention_grads",
    )(*operands)


def finish_kernel(n_chunks, paired, chained, start, flag_ref, *refs):
    dk_ref, dv_ref = refs[-2:]
    per_chunk = (len(refs) - 2 - (2 if chained else 0)) // n_chunks
    w = HEAD_WIDTH
    at = start
    for i in range(n_chunks):
        own_ref, *term_refs = refs[i * per_chunk : (i + 1) * per_chunk]
        for h in range(own_ref.shape[1] // (2 * w)):
            cols = slice(2 * h * w, 2 * (h + 1) * w)
            total = own_ref[:, cols]
            for t, ref in enumerate(term_refs):
                term = ref[:, cols].astype(jnp.float32)
                if paired and t == 1:
                    term = jnp.where(flag_ref[0, 0] == 1, 0.0, term)
                total = total + term
            dk_ref[:, at : at + w] = total[:, :w].astype(dk_ref.dtype)
            dv_ref[:, at : at + w] = total[:, w:].astype(dv_ref.dtype)
            at += w


def finished(flag, paired, parts, first, shape, before):
    rows = shape[0]
    w = HEAD_WIDTH
    scalars = pl.BlockSpec(memory_space=pltpu.SMEM)
    step = min(rows, BLOCK)
    if before is None:
        grid = (rows // step,)
        arrays = [x for part in parts for x in part]
        in_specs = [pl.BlockSpec((step, x.shape[1]), lambda r: (r, 0)) for x in arrays]
        out_spec = pl.BlockSpec((step, shape[1]), lambda r: (r, 0))
        aliases = {}
        start = first * w
    else:
        arrays = list(parts[0])
        grid = (arrays[0].shape[1] // (2 * w),)
        in_specs = [pl.BlockSpec((rows, 2 * w), lambda h: (0, h))] * len(arrays)
        out_spec = pl.BlockSpec((rows, w), lambda h: (0, first + h))
        aliases = {len(arrays) + 1: 0, len(arrays) + 2: 1}
        arrays += list(before)
        in_specs += [pl.BlockSpec(memory_space=pl.ANY)] * 2
        start = 0
    return pl.pallas_call(
        functools.partial(finish_kernel, len(parts), paired, before is not None, start),
        out_shape=[jax.ShapeDtypeStruct(shape, jnp.bfloat16)] * 2,
        grid=grid,
        in_specs=[scalars] + in_specs,
        out_specs=[out_spec] * 2,
        input_output_aliases=aliases,
        compiler_params=pltpu.CompilerParams(vmem_limit_bytes=48 * 1024 * 1024),
        cost_estimate=pl.CostEstimate(flops=1_000_000, bytes_accessed=1, transcendentals=0),
        name="sum_key_value_grads",
    )(flag, *arrays)


def gate_kernel(flag_ref, *refs):
    refs[-1][0, 0] = flag_ref[0, 0]


def gated(flag, after):
    scalars = pl.BlockSpec(memory_space=pltpu.SMEM)
    return pl.pallas_call(
        gate_kernel,
        out_shape=jax.ShapeDtypeStruct(flag.shape, flag.dtype),
        in_specs=[scalars] + [pl.BlockSpec(memory_space=pl.ANY)] * len(after),
        out_specs=scalars,
        cost_estimate=pl.CostEstimate(flops=30_000_000_000, bytes_accessed=1, transcendentals=0),
        name="wait_for_returns",
    )(flag, *after)


def chunk_heads(kv_heads):
    total = sum(CHUNK_SHARES)
    if kv_heads % total:
        return [kv_heads]
    return [share * kv_heads // total for share in CHUNK_SHARES]


def on_device(query, key, value, out_grad, block_mask):
    rows = query.shape[0]
    kv_heads = key.shape[1] // HEAD_WIDTH
    n_pieces = WINDOW // rows
    n_head = lax.axis_size("head")
    device = lax.axis_index("ctx") * n_head + lax.axis_index("head")
    first_block = device * (rows // BLOCK)
    own_rows = lax.dynamic_slice_in_dim(block_mask, first_block, rows // BLOCK, 0)
    block = first_block + lax.broadcasted_iota(jnp.int32, own_rows.shape, 0)
    offset = lax.broadcasted_iota(jnp.int32, own_rows.shape, 1)
    usable = (own_rows > 0) & (block >= offset)
    bias = jnp.where(usable, 0.0, -jnp.inf).astype(jnp.float32)
    paired = n_pieces == 2 and n_head % 2 == 0
    flag = lax.rem(device, 2).astype(jnp.int32).reshape(1, 1)
    bf16 = jnp.bfloat16
    f32 = jnp.float32

    counts = chunk_heads(kv_heads)
    n_chunks = len(counts)
    firsts = [sum(counts[:i]) for i in range(n_chunks)]
    packs = packed(key, value, 0, counts[:1], [])
    if n_chunks > 1:
        packs += packed(key, value, counts[0], counts[1:], packs)
    if paired:
        far = [moved(x, 2) for x in packs]
    else:
        far = [[moved(x, j) for j in range(n_pieces, 0, -1)] for x in packs]

    def offer(i):
        early = [far[j] for at, j in ARRIVALS if at == i and j < n_chunks]
        ready = gated(flag, early) if early else flag
        return jnp.where(ready[0, 0] == 1, far[i], packs[i])

    def settle(i):
        back = GATES[min(i, len(GATES) - 1)]
        ready = gated(flag, terms[back][:1]) if 0 <= back < i else flag
        odd = ready[0, 0] == 1
        d_far, from_pair = waiting[i]
        for_far = d_far.astype(f32) + jnp.where(odd, from_pair, 0).astype(f32)
        for_far = for_far.astype(bf16)
        terms.append([moved(for_far, -2), from_pair])
        return for_far

    dq = None
    owns, terms, waiting, offers, nears = [], [], [], [], []
    for i in range(n_chunks):
        after = []
        if paired:
            n_offers, n_settled, n_back = (min(x, n_chunks) for x in ORDER[min(i, len(ORDER) - 1)])
            for j in range(len(offers), max(n_offers, i + 1)):
                offers.append(offer(j))
                nears.append(swapped(offers[j]))
                after.append(offers[j])
            for j in range(len(terms), min(n_settled, i)):
                after.append(settle(j))
            after += [term[0] for term in terms[:n_back]]
        pieces = [far[i], nears[i]] if paired else far[i]
        dq, flag, own, *d_pieces = attention(
            flag, bias, query, out_grad, key, value, pieces, firsts[i], counts[i], dq, after
        )
        owns.append(own)
        if paired:
            waiting.append([d_pieces[0], swapped(d_pieces[1])])
        else:
            terms.append([moved(x, j - n_pieces) for j, x in enumerate(d_pieces)])
    if paired:
        for i in range(len(terms), n_chunks):
            settle(i)
    parts = [[own, *term] for own, term in zip(owns, terms)]
    early = max(1, n_chunks - 2)
    grads = finished(flag, paired, parts[:early], 0, key.shape, None)
    for i in range(early, n_chunks):
        grads = finished(flag, paired, parts[i : i + 1], firsts[i], key.shape, grads)
    return (dq, grads[0], grads[1])


def solution(mesh):
    split = P(("ctx", "head"), None)
    return jax.shard_map(
        on_device,
        mesh=mesh,
        in_specs=(split, split, split, split, P()),
        out_specs=(split, split, split),
        check_vma=False,
    )
```

```python
import functools
import math

import jax
import jax.numpy as jnp
from jax import lax
from jax.experimental import pallas as pl
from jax.experimental.pallas import tpu as pltpu
from jax.sharding import PartitionSpec as P

HEAD_WIDTH = 128
WINDOW = 1024
BLOCK = 128
PRE_SCALE = 168.0 ** (-0.5)
LOG2_SCALE = PRE_SCALE * math.log2(math.e)
AXES = ("ctx", "head")
CHUNK_SHARES = (4, 4, 4, 2, 2)
HEADS_PER_STEP = 1
ORDER = ((2, 0, 0), (3, 0, 0), (4, 1, 0), (5, 2, 1), (5, 3, 2))
GATES = (-1, -1, -1, -1, 2)
NT = (((1,), (1,)), ((), ()))
NN = (((1,), (0,)), ((), ()))


def moved(block, distance):
    n = lax.axis_size(AXES[0]) * lax.axis_size(AXES[1])
    route = [(i, i + distance) for i in range(n) if 0 <= i + distance < n]
    return lax.ppermute(block, AXES, route)


def swapped(block):
    n = lax.axis_size(AXES[0]) * lax.axis_size(AXES[1])
    return lax.ppermute(block, AXES, [(i, i ^ 1) for i in range(n)])


def pack_kernel(first, counts, k_ref, v_ref, *refs):
    w = HEAD_WIDTH
    at = first
    for heads, out_ref in zip(counts, refs[-len(counts) :]):
        for h in range(heads):
            source = slice((at + h) * w, (at + h + 1) * w)
            out_ref[:, 2 * h * w : (2 * h + 1) * w] = k_ref[:, source]
            out_ref[:, (2 * h + 1) * w : (2 * h + 2) * w] = v_ref[:, source]
        at += heads


def packed(key, value, first, counts, after):
    rows = key.shape[0]
    step = min(rows, BLOCK)
    spec = pl.BlockSpec((step, (first + sum(counts)) * HEAD_WIDTH), lambda r: (r, 0))
    widths = [2 * HEAD_WIDTH * heads for heads in counts]
    return pl.pallas_call(
        functools.partial(pack_kernel, first, counts),
        out_shape=[jax.ShapeDtypeStruct((rows, x), key.dtype) for x in widths],
        grid=(rows // step,),
        in_specs=[spec, spec] + [pl.BlockSpec(memory_space=pl.ANY)] * len(after),
        out_specs=[pl.BlockSpec((step, x), lambda r: (r, 0)) for x in widths],
        name="pack_key_value",
    )(key, value, *after)


def dot(a, b, dims):
    return lax.dot_general(a, b, dims, preferred_element_type=jnp.float32)


def attention_kernel(n_pieces, per_group, per_step, n_extra, *refs):
    flag_ref, bias_ref, q_ref, g_ref, k_ref, v_ref = refs[:6]
    piece_refs = refs[6 : 6 + n_pieces]
    rest = refs[6 + n_pieces + n_extra :]
    dq_ref, flag_out_ref, down_ref = rest[:3]
    dpiece_refs = rest[3 : 3 + n_pieces]
    k_ext, v_ext, k_turned, q_all, g_all, q_low, g_low, p_all, ds_all = rest[3 + n_pieces :]
    flag_out_ref[0, 0] = flag_ref[0, 0]
    rows = q_ref.shape[0]
    tiles = rows // BLOCK
    lead = n_pieces * rows
    wide = per_group * BLOCK
    span = WINDOW + BLOCK
    n_off = span // BLOCK
    w = HEAD_WIDTH
    bf16 = jnp.bfloat16

    for s in range(per_step):
        for i, piece in enumerate(piece_refs):
            k_ext[s, i * rows : (i + 1) * rows, :] = piece[:, 2 * s * w : (2 * s + 1) * w]
            v_ext[s, i * rows : (i + 1) * rows, :] = piece[:, (2 * s + 1) * w : (2 * s + 2) * w]
        k_ext[s, lead:, :] = k_ref[:, s * w : (s + 1) * w]
        v_ext[s, lead:, :] = v_ref[:, s * w : (s + 1) * w]
        k_turned[s] = k_ext[s].T
        for b in range(tiles):
            for r in range(per_group):
                at = b * wide + r * BLOCK
                source = (
                    slice(b * BLOCK, (b + 1) * BLOCK),
                    slice((s * per_group + r) * w, (s * per_group + r + 1) * w),
                )
                q_all[s, at : at + BLOCK, :] = q_ref[source]
                g_all[s, at : at + BLOCK, :] = g_ref[source]

    k_index = lax.broadcasted_iota(jnp.int32, (BLOCK, wide), 0)
    q_index = lax.rem(lax.broadcasted_iota(jnp.int32, (BLOCK, wide), 1), BLOCK)
    lower = k_index <= q_index
    group = span
    units = [(s, b) for s in range(per_step) for b in range(tiles)]

    def group_steps(u, key_ref, query_ref, parts):
        s, b = units[u]

        def one(start):
            top = b * BLOCK + start
            out = dot(key_ref[s, top : top + group, :], query_ref[s, b * wide : (b + 1) * wide, :], NT)
            parts.extend(out[i * BLOCK : (i + 1) * BLOCK] for i in range(group // BLOCK))

        return [functools.partial(one, start) for start in range(0, span, group)]

    def folded(x, op):
        return op(x.reshape(BLOCK // 8, 8, wide), axis=0)

    def edge_first(parts, bias0):
        first = parts[0] if bias0 is None else parts[0] + bias0
        return [jnp.where(lower, parts[-1], first)] + parts[1:-1]

    def key_steps(s):
        n_key = (lead + rows) // BLOCK
        steps = []

        def one(j, end, low, high):
            here = slice(j * BLOCK, end * BLOCK)
            cols = slice(low * wide, (high + 1) * wide)
            dv = dot(p_all[s, here, cols], g_low[s, cols, :], NN)
            dk = dot(ds_all[s, here, cols], q_low[s, cols, :], NN) * PRE_SCALE
            for i in range(j, end):
                target = down_ref if i * BLOCK >= lead else dpiece_refs[i * BLOCK // rows]
                there = slice(i * BLOCK % rows, i * BLOCK % rows + BLOCK)
                part = slice((i - j) * BLOCK, (i - j + 1) * BLOCK)
                target[there, 2 * s * w : (2 * s + 1) * w] = dk[part].astype(target.dtype)
                target[there, (2 * s + 1) * w : (2 * s + 2) * w] = dv[part].astype(target.dtype)

        j = 0
        while j < n_key:
            use = max(0, j - n_off + 1), min(tiles - 1, j)
            end = j + 1
            while end < n_key and (max(0, end - n_off + 1), min(tiles - 1, end)) == use:
                end += 1
            steps.append(functools.partial(one, j, end, *use))
            j = end
        return steps

    pending = []
    scores = [[] for _ in units]
    d_probs = [[] for _ in units]
    for step in group_steps(0, k_ext, q_all, scores[0]) + group_steps(0, v_ext, g_all, d_probs[0]):
        step()

    for u, (s, b) in enumerate(units):
        top = b * BLOCK
        cols = slice(b * wide, (b + 1) * wide)
        ahead = group_steps(u + 1, k_ext, q_all, scores[u + 1]) if u + 1 < len(units) else []
        later = group_steps(u + 1, v_ext, g_all, d_probs[u + 1]) if u + 1 < len(units) else []
        bias = [bias_ref[b, n_off - 1 - i] for i in range(n_off - 1)]
        parts = edge_first(scores[u], bias[0])
        shifts = [None] + bias[1:]
        best = folded(parts[0], jnp.max)
        for part, shift in zip(parts[1:], shifts[1:]):
            best = jnp.maximum(best, folded(part, jnp.max) + shift)
        best = jnp.max(best, axis=0, keepdims=True) * LOG2_SCALE
        d_parts = edge_first(d_probs[u], None)
        total = jnp.zeros((8, wide), jnp.float32)
        moment = jnp.zeros((8, wide), jnp.float32)
        weights = []
        for i, (part, d_part, shift) in enumerate(zip(parts, d_parts, shifts)):
            if i % 3 == 0 and ahead:
                ahead.pop(0)()
            if i % 3 == 1 and pending:
                pending.pop(0)()
            x = jnp.exp2(part * LOG2_SCALE - (best if shift is None else best - shift))
            weights.append(x)
            total = total + folded(x, jnp.sum)
            moment = moment + folded(x * d_part, jnp.sum)
            if i == 0:
                p_all[s, top : top + BLOCK, cols] = jnp.where(lower, 0.0, x).astype(bf16)
                p_all[s, top + WINDOW : top + span, cols] = jnp.where(lower, x, 0.0).astype(bf16)
            else:
                p_all[s, top + i * BLOCK : top + (i + 1) * BLOCK, cols] = x.astype(bf16)
        for step in ahead:
            step()
        inverse = 1.0 / jnp.sum(total, axis=0, keepdims=True)
        delta = jnp.sum(moment, axis=0, keepdims=True) * inverse
        column = jnp.broadcast_to(inverse, (8, wide)).T[:, :1]
        q_low[s, cols, :] = (q_all[s, cols, :].astype(jnp.float32) * column).astype(bf16)
        g_low[s, cols, :] = (g_all[s, cols, :].astype(jnp.float32) * column).astype(bf16)
        for i, (x, d_part) in enumerate(zip(weights, d_parts)):
            if i % 3 == 0 and later:
                later.pop(0)()
            if i % 3 == 1 and pending:
                pending.pop(0)()
            d_score = x * (d_part - delta)
            if i == 0:
                ds_all[s, top : top + BLOCK, cols] = jnp.where(lower, 0.0, d_score).astype(bf16)
                ds_all[s, top + WINDOW : top + span, cols] = jnp.where(lower, d_score, 0.0).astype(
                    bf16
                )
            else:
                ds_all[s, top + i * BLOCK : top + (i + 1) * BLOCK, cols] = d_score.astype(bf16)
        for step in later:
            step()
        scores[u] = d_probs[u] = None

        def query_step(s=s, top=top, cols=cols, inverse=inverse):
            turned = dot(k_turned[s, :, top : top + span], ds_all[s, top : top + span, cols], NN)
            dq_two = (turned * (inverse * PRE_SCALE)).T
            for r in range(per_group):
                at = (s * per_group + r) * w
                dq_ref[top : top + BLOCK, at : at + w] = dq_two[
                    r * BLOCK : (r + 1) * BLOCK
                ].astype(dq_ref.dtype)

        pending.append(query_step)
        if b == tiles - 1:
            pending += key_steps(s)
    for step in pending:
        step()


def attention(flag, bias, query, out_grad, key, value, pieces, first, heads, dq_before, after):
    rows = query.shape[0]
    per_group = query.shape[1] // key.shape[1]
    n = len(pieces)
    w = HEAD_WIDTH
    per_step = next(x for x in (HEADS_PER_STEP, 1) if heads % x == 0 and first % x == 0)
    at = first // per_step
    q_spec = pl.BlockSpec((rows, per_step * per_group * w), lambda h: (0, at + h))
    k_spec = pl.BlockSpec((rows, per_step * w), lambda h: (0, at + h))
    kv_spec = pl.BlockSpec((rows, per_step * 2 * w), lambda h: (0, h))
    scalars = pl.BlockSpec(memory_space=pltpu.SMEM)
    in_specs = [scalars, scalars, q_spec, q_spec, k_spec, k_spec] + [kv_spec] * n
    operands = [flag, bias, query, out_grad, key, value, *pieces]
    aliases = {}
    if dq_before is not None:
        aliases = {len(operands): 0}
        operands.append(dq_before)
    operands += after
    n_extra = len(operands) - len(in_specs)
    in_specs += [pl.BlockSpec(memory_space=pl.ANY)] * n_extra
    kv_shape = (rows, heads * 2 * w)
    length = (n + 1) * rows
    wide = rows * per_group
    bf16 = jnp.bfloat16
    return pl.pallas_call(
        functools.partial(attention_kernel, n, per_group, per_step, n_extra),
        out_shape=[
            jax.ShapeDtypeStruct(query.shape, query.dtype),
            jax.ShapeDtypeStruct(flag.shape, flag.dtype),
            jax.ShapeDtypeStruct(kv_shape, jnp.float32),
        ]
        + [jax.ShapeDtypeStruct(kv_shape, bf16)] * n,
        grid=(heads // per_step,),
        in_specs=in_specs,
        out_specs=[q_spec, scalars] + [kv_spec] * (n + 1),
        scratch_shapes=[
            pltpu.VMEM((per_step, length, w), bf16),
            pltpu.VMEM((per_step, length, w), bf16),
            pltpu.VMEM((per_step, w, length), bf16),
            pltpu.VMEM((per_step, wide, w), bf16),
            pltpu.VMEM((per_step, wide, w), bf16),
            pltpu.VMEM((per_step, wide, w), bf16),
            pltpu.VMEM((per_step, wide, w), bf16),
            pltpu.VMEM((per_step, length, wide), bf16),
            pltpu.VMEM((per_step, length, wide), bf16),
        ],
        input_output_aliases=aliases,
        compiler_params=pltpu.CompilerParams(vmem_limit_bytes=56 * 1024 * 1024),
        cost_estimate=pl.CostEstimate(flops=heads * 6_000_000_000, bytes_accessed=1, transcendentals=0),
        name="attention_grads",
    )(*operands)


def finish_kernel(n_chunks, paired, chained, start, flag_ref, *refs):
    dk_ref, dv_ref = refs[-2:]
    per_chunk = (len(refs) - 2 - (2 if chained else 0)) // n_chunks
    w = HEAD_WIDTH
    at = start
    for i in range(n_chunks):
        own_ref, *term_refs = refs[i * per_chunk : (i + 1) * per_chunk]
        for h in range(own_ref.shape[1] // (2 * w)):
            cols = slice(2 * h * w, 2 * (h + 1) * w)
            total = own_ref[:, cols]
            for t, ref in enumerate(term_refs):
                term = ref[:, cols].astype(jnp.float32)
                if paired and t == 1:
                    term = jnp.where(flag_ref[0, 0] == 1, 0.0, term)
                total = total + term
            dk_ref[:, at : at + w] = total[:, :w].astype(dk_ref.dtype)
            dv_ref[:, at : at + w] = total[:, w:].astype(dv_ref.dtype)
            at += w


def finished(flag, paired, parts, first, shape, before):
    rows = shape[0]
    w = HEAD_WIDTH
    scalars = pl.BlockSpec(memory_space=pltpu.SMEM)
    step = min(rows, BLOCK)
    if before is None:
        grid = (rows // step,)
        arrays = [x for part in parts for x in part]
        in_specs = [pl.BlockSpec((step, x.shape[1]), lambda r: (r, 0)) for x in arrays]
        out_spec = pl.BlockSpec((step, shape[1]), lambda r: (r, 0))
        aliases = {}
        start = first * w
    else:
        arrays = list(parts[0])
        grid = (arrays[0].shape[1] // (2 * w),)
        in_specs = [pl.BlockSpec((rows, 2 * w), lambda h: (0, h))] * len(arrays)
        out_spec = pl.BlockSpec((rows, w), lambda h: (0, first + h))
        aliases = {len(arrays) + 1: 0, len(arrays) + 2: 1}
        arrays += list(before)
        in_specs += [pl.BlockSpec(memory_space=pl.ANY)] * 2
        start = 0
    return pl.pallas_call(
        functools.partial(finish_kernel, len(parts), paired, before is not None, start),
        out_shape=[jax.ShapeDtypeStruct(shape, jnp.bfloat16)] * 2,
        grid=grid,
        in_specs=[scalars] + in_specs,
        out_specs=[out_spec] * 2,
        input_output_aliases=aliases,
        compiler_params=pltpu.CompilerParams(vmem_limit_bytes=48 * 1024 * 1024),
        cost_estimate=pl.CostEstimate(flops=1_000_000, bytes_accessed=1, transcendentals=0),
        name="sum_key_value_grads",
    )(flag, *arrays)


def gate_kernel(flag_ref, *refs):
    refs[-1][0, 0] = flag_ref[0, 0]


def gated(flag, after):
    scalars = pl.BlockSpec(memory_space=pltpu.SMEM)
    return pl.pallas_call(
        gate_kernel,
        out_shape=jax.ShapeDtypeStruct(flag.shape, flag.dtype),
        in_specs=[scalars] + [pl.BlockSpec(memory_space=pl.ANY)] * len(after),
        out_specs=scalars,
        cost_estimate=pl.CostEstimate(flops=1, bytes_accessed=1, transcendentals=0),
        name="wait_for_returns",
    )(flag, *after)


def chunk_heads(kv_heads):
    total = sum(CHUNK_SHARES)
    if kv_heads % total:
        return [kv_heads]
    return [share * kv_heads // total for share in CHUNK_SHARES]


def on_device(query, key, value, out_grad, block_mask):
    rows = query.shape[0]
    kv_heads = key.shape[1] // HEAD_WIDTH
    n_pieces = WINDOW // rows
    n_head = lax.axis_size("head")
    device = lax.axis_index("ctx") * n_head + lax.axis_index("head")
    first_block = device * (rows // BLOCK)
    own_rows = lax.dynamic_slice_in_dim(block_mask, first_block, rows // BLOCK, 0)
    block = first_block + lax.broadcasted_iota(jnp.int32, own_rows.shape, 0)
    offset = lax.broadcasted_iota(jnp.int32, own_rows.shape, 1)
    usable = (own_rows > 0) & (block >= offset)
    bias = jnp.where(usable, 0.0, -jnp.inf).astype(jnp.float32)
    paired = n_pieces == 2 and n_head % 2 == 0
    flag = lax.rem(device, 2).astype(jnp.int32).reshape(1, 1)
    bf16 = jnp.bfloat16
    f32 = jnp.float32

    counts = chunk_heads(kv_heads)
    n_chunks = len(counts)
    firsts = [sum(counts[:i]) for i in range(n_chunks)]
    packs = packed(key, value, 0, counts[:1], [])
    if n_chunks > 1:
        packs += packed(key, value, counts[0], counts[1:], packs)
    if paired:
        far = [moved(x, 2) for x in packs]
    else:
        far = [[moved(x, j) for j in range(n_pieces, 0, -1)] for x in packs]

    def offer(i):
        return jnp.where(flag[0, 0] == 1, far[i], packs[i])

    def settle(i):
        back = GATES[min(i, len(GATES) - 1)]
        ready = gated(flag, terms[back][:1]) if 0 <= back < i else flag
        odd = ready[0, 0] == 1
        d_far, from_pair = waiting[i]
        for_far = d_far.astype(f32) + jnp.where(odd, from_pair, 0).astype(f32)
        for_far = for_far.astype(bf16)
        terms.append([moved(for_far, -2), from_pair])
        return for_far

    dq = None
    owns, terms, waiting, offers, nears = [], [], [], [], []
    for i in range(n_chunks):
        after = []
        if paired:
            n_offers, n_settled, n_back = (min(x, n_chunks) for x in ORDER[min(i, len(ORDER) - 1)])
            for j in range(len(offers), max(n_offers, i + 1)):
                offers.append(offer(j))
                nears.append(swapped(offers[j]))
                after.append(offers[j])
            for j in range(len(terms), min(n_settled, i)):
                after.append(settle(j))
            after += [term[0] for term in terms[:n_back]]
        pieces = [far[i], nears[i]] if paired else far[i]
        dq, flag, own, *d_pieces = attention(
            flag, bias, query, out_grad, key, value, pieces, firsts[i], counts[i], dq, after
        )
        owns.append(own)
        if paired:
            waiting.append([d_pieces[0], swapped(d_pieces[1])])
        else:
            terms.append([moved(x, j - n_pieces) for j, x in enumerate(d_pieces)])
    if paired:
        for i in range(len(terms), n_chunks):
            settle(i)
    parts = [[own, *term] for own, term in zip(owns, terms)]
    early = max(1, n_chunks - 2)
    grads = finished(flag, paired, parts[:early], 0, key.shape, None)
    for i in range(early, n_chunks):
        grads = finished(flag, paired, parts[i : i + 1], firsts[i], key.shape, grads)
    return (dq, grads[0], grads[1])


def solution(mesh):
    split = P(("ctx", "head"), None)
    return jax.shard_map(
        on_device,
        mesh=mesh,
        in_specs=(split, split, split, split, P()),
        out_specs=(split, split, split),
        check_vma=False,
    )
```
